32 devices in a mesh: gr: 8 (over y, x, core), gc: 4 (over z).
Axes of the slice: x: 2, y: 2, z: 4, core: 2. Of those that a mesh axis runs over, the one named last changes fastest.
Arguments:
- child_rows: float32 [4096, 12288], P('gr', 'gc'), may hold values from -1.5 to 1.5
- row_map: int32 [4096], P('gr'), may hold values from 0 to 4095, as said below
- stair: int32 [32], replicated, may hold values from 0 to 896, as said below
Outputs:
- factor: float32 [1024, 12288], P('gr', 'gc')
- projected: float32 [4096, 12288], P('gr', 'gc')
The draws below stay inside these ranges and needn't reach their ends.
Inputs may be any that keep to these rules, and one draw needn't show every extreme that they name: row_map is a permutation of 0 to 4095. Of the 512 rows of one index of gr, at most 176 go to the rows of any one index of gr (row_map // 512), and some index of gr sends exactly 176 to one index. stair is nondecreasing and a multiple of 128; the first quarter of the blocks is 0 and the last block holds 896.
All inputs are finite; a program needn't handle non-finite values.
Results may differ from the reference program's by a relative error of at most 0.0003.
Values sent between devices are 32-bit elements; how exact they have to be, the bound alone decides.
No kernel may reach another device: no remote copies, remote signals or barrier semaphores. Data moves between devices by JAX's collectives and lax.ppermute only.
A program may use at most 128 MiB of HBM per device.

```python
import jax
import jax.numpy as jnp
from jax import lax

NCOL = 12288
PANEL = 512
NPANEL = 2
STAIR_BLOCK = 128
ROWS_DEV = 512
ROWS = 4096
BLOCKS = 32
BASE = 48
N_GR = 8


def draw_row_map(key, part):
    key_pair, key_order, key_slot = jax.random.split(jax.random.fold_in(key, 11), 3)
    pairing = jax.random.permutation(key_pair, N_GR).astype(jnp.int32)
    heavy = ROWS_DEV - BASE * N_GR
    base_dest = jnp.repeat(jnp.arange(N_GR, dtype=jnp.int32), BASE)
    spread_part = jnp.broadcast_to(base_dest[None, :], (N_GR, BASE * N_GR))
    heavy_part = jnp.broadcast_to(pairing[:, None], (N_GR, heavy))
    targets = jnp.concatenate([spread_part, heavy_part], axis=1)
    iota_rows = jnp.arange(ROWS_DEV, dtype=jnp.int32)[None, :]
    scores = jax.random.randint(key_order, (N_GR, ROWS_DEV), 0, 1048576) * ROWS_DEV + iota_rows
    order = jnp.argsort(scores, axis=1)
    targets = jnp.take_along_axis(targets, order, axis=1)
    flat_dest = targets.reshape(-1)
    onehot = (flat_dest[:, None] == jnp.arange(N_GR, dtype=jnp.int32)[None, :]).astype(jnp.int32)
    rank_within = jnp.sum((jnp.cumsum(onehot, axis=0) - onehot) * onehot, axis=1)
    slot_scores = jax.random.randint(key_slot, (N_GR, ROWS_DEV), 0, 1048576) * ROWS_DEV + iota_rows
    slot_perm = jnp.argsort(slot_scores, axis=1).astype(jnp.int32)
    target_row = slot_perm[flat_dest, rank_within]
    return (flat_dest * ROWS_DEV + target_row).astype(jnp.int32)


def draw_stair(key, part):
    levels = 2 * PANEL // STAIR_BLOCK - 1
    values = jax.random.randint(jax.random.fold_in(key, 23), (BLOCKS,), 0, levels + 1)
    values = jnp.sort(values)
    block_ids = jnp.arange(BLOCKS, dtype=jnp.int32)
    values = jnp.where(block_ids < BLOCKS // 4, 0, values)
    values = jnp.where(block_ids == BLOCKS - 1, levels, values)
    return (values * STAIR_BLOCK).astype(jnp.int32)


def steps_of(own_key, shape, shards, smallest, largest):
    factor_of, own = 1.0, jax.random.fold_in(own_key, 6)
    for dim, shards_of in shards:
        draws = jnp.exp(jax.random.uniform(jax.random.fold_in(own, dim), (shards_of,), jnp.float32, smallest / len(shards), largest / len(shards)))
        factor_of = factor_of * jnp.repeat(draws, shape[dim] // shards_of).reshape([-1 if axis == dim else 1 for axis in range(len(shape))])
    return factor_of


def bell_draw(stream_key, dims, spread, most, cuts=(), held_as=jnp.bfloat16):
    values = jax.random.normal(stream_key, dims, jnp.float32) * spread
    if len(cuts) > 0:
        values = steps_of(stream_key, dims, cuts, -0.22, 0.18) * values
    return jnp.clip(values, min=-most, max=most).astype(held_as)


def setup_inputs(seed: int = 0) -> dict:
    key_list = jax.random.split(jax.random.key(seed), 4)
    child_rows = bell_draw(key_list[0], (ROWS, NCOL), 0.25, 1.5, ((0, 8), (1, 4)), jnp.float32)
    row_map = draw_row_map(jax.random.fold_in(key_list[3], 71), 0)
    stair = draw_stair(jax.random.fold_in(key_list[3], 71), 0)
    return dict(child_rows=child_rows, row_map=row_map, stair=stair)


def reference(child_rows, row_map, stair):
    front = jnp.zeros_like(child_rows).at[row_map].set(child_rows)
    row_ids = jnp.arange(front.shape[0], dtype=jnp.int32)
    col_ids = jnp.arange(front.shape[1], dtype=jnp.int32)
    limits = jnp.take(stair, row_ids // STAIR_BLOCK)
    front_work = jnp.where(col_ids[None, :] >= limits[:, None], front, jnp.zeros_like(front))
    blocks = []
    for step in range(NPANEL):
        panel_block = front_work[:, step * PANEL:(step + 1) * PANEL]
        basis_cols, triangle = jnp.linalg.qr(panel_block)
        signs = jnp.where(jnp.diagonal(triangle) < 0, -1.0, 1.0).astype(front_work.dtype)
        basis_cols = basis_cols * signs[None, :]
        coupling = jnp.dot(basis_cols.T.astype(jnp.float32), front_work.astype(jnp.float32), precision=lax.Precision.HIGHEST, preferred_element_type=jnp.float32)
        front_work = front_work - jnp.dot(basis_cols.astype(jnp.float32), coupling.astype(jnp.float32), precision=lax.Precision.HIGHEST, preferred_element_type=jnp.float32)
        blocks.append(coupling)
    return (jnp.concatenate(blocks, axis=0), front_work)
```

```python
import jax
import jax.numpy as jnp
from jax import lax
from jax.experimental import pallas as pl
from jax.experimental.pallas import tpu as pltpu
from jax.sharding import PartitionSpec as P

PANEL = 512
NPANEL = 2
STAIR_BLOCK = 128
EDGE = 128
HIGHEST = lax.Precision.HIGHEST
HIGH = lax.Precision.HIGH


def dot(left, right, dims, precision):
    return lax.dot_general(
        left, right, (dims, ((), ())), precision=precision, preferred_element_type=jnp.float32
    )


def eliminate(tiles):
    lane = lax.broadcasted_iota(jnp.int32, (8, EDGE), 1)
    sub = lax.broadcasted_iota(jnp.int32, (8, EDGE), 0)
    tiles = list(tiles)
    strips = len(tiles)
    for strip in range(strips):
        first = 8 * strip
        own = (lane >= first) & (lane < first + 8)
        mult = {
            t: [jnp.broadcast_to(tiles[t][:, first + s : first + s + 1], (8, EDGE)) for s in range(8)]
            for t in range(strip, strips)
        }
        small = [
            [jnp.broadcast_to(mult[strip][s][t : t + 1, :], (8, EDGE)) for s in range(t + 1)]
            for t in range(8)
        ]
        start = jnp.where(own, jnp.where(lane - first == sub, 1.0, 0.0), tiles[strip])
        rows = [jnp.broadcast_to(start[s : s + 1, :], (8, EDGE)) for s in range(8)]
        inv = [None] * 8
        low = [[None] * 8 for _ in range(8)]
        for s in range(8):
            inv[s] = 1.0 / small[s][s]
            for t in range(s + 1, 8):
                low[t][s] = small[t][s] * inv[s]
                for u in range(s + 1, t + 1):
                    small[t][u] = small[t][u] - low[t][s] * small[u][s]
            for t in range(s + 1, 8):
                rows[t] = rows[t] - low[t][s] * rows[s]
        back = [None] * 8
        for s in range(7, -1, -1):
            value = rows[s] * inv[s]
            for t in range(7, s, -1):
                value = value - low[t][s] * back[t]
            back[s] = value
        out, pivot = rows[7], small[7][7]
        for s in range(6, -1, -1):
            out = jnp.where(sub == s, rows[s], out)
            pivot = jnp.where(sub == s, small[s][s], pivot)
        tiles[strip] = out * lax.rsqrt(pivot)
        for t in range(strip + 1, strips):
            value = jnp.where(own, 0.0, tiles[t])
            for s in range(8):
                value = value - mult[t][s] * back[s]
            tiles[t] = value
    return tiles


def inverse_factor_kernel(gram_ref, out_ref, work):
    size = gram_ref.shape[0]
    blocks = size // EDGE
    work[...] = gram_ref[...]
    out_ref[...] = jnp.zeros_like(out_ref)
    lower = lax.broadcasted_iota(jnp.int32, (EDGE, EDGE), 0) >= lax.broadcasted_iota(
        jnp.int32, (EDGE, EDGE), 1
    )

    @pl.loop(0, blocks)
    def _(k):
        at = pl.multiple_of(k * EDGE, EDGE)
        tiles = [
            work[pl.ds(pl.multiple_of(at + 8 * t, 8), 8), pl.ds(at, EDGE)] for t in range(EDGE // 8)
        ]
        diag = jnp.where(lower, jnp.concatenate(eliminate(tiles), axis=0), 0.0)
        work[pl.ds(at, EDGE), :] = dot(diag, work[pl.ds(at, EDGE), :], ((1,), (0,)), HIGHEST)
        work[pl.ds(at, EDGE), pl.ds(at, EDGE)] = diag

        @pl.loop(k + 1, blocks)
        def _(i):
            below = pl.multiple_of(i * EDGE, EDGE)
            coeff = work[pl.ds(at, EDGE), pl.ds(below, EDGE)]
            work[pl.ds(below, EDGE), pl.ds(at, EDGE)] = jnp.zeros((EDGE, EDGE), jnp.float32)
            work[pl.ds(below, EDGE), :] -= dot(coeff, work[pl.ds(at, EDGE), :], ((0,), (0,)), HIGHEST)

        @pl.loop(0, k + 1)
        def _(j):
            left = pl.multiple_of(j * EDGE, EDGE)
            out_ref[pl.ds(at, EDGE), pl.ds(left, EDGE)] = work[pl.ds(at, EDGE), pl.ds(left, EDGE)]


def inverse_factor(gram):
    size = gram.shape[0]
    return pl.pallas_call(
        inverse_factor_kernel,
        out_shape=jax.ShapeDtypeStruct((size, size), jnp.float32),
        in_specs=[pl.BlockSpec(memory_space=pltpu.VMEM)],
        out_specs=pl.BlockSpec(memory_space=pltpu.VMEM),
        scratch_shapes=[pltpu.VMEM((size, size), jnp.float32)],
        compiler_params=pltpu.CompilerParams(vmem_limit_bytes=40 * 2**20),
        cost_estimate=pl.CostEstimate(
            flops=6 * 2 * size**3, bytes_accessed=8 * size * size, transcendentals=size
        ),
        name="inverse_factor",
    )(gram)


def pick(where_to, count):
    rows = lax.broadcasted_iota(jnp.int32, (count, where_to.shape[1]), 0)
    return jnp.where(rows == where_to, 1.0, 0.0).astype(jnp.bfloat16)


def move(matrix, values):
    high = values.astype(jnp.bfloat16)
    rest = (values - high.astype(jnp.float32)).astype(jnp.bfloat16)
    dims = ((1,), (0,))
    return dot(matrix, high, dims, None) + dot(matrix, rest, dims, None)


def reorder_kernel(to_ref, in_ref, out_ref, matrix):
    @pl.when(pl.program_id(0) == 0)
    def _():
        matrix[...] = pick(to_ref[...], matrix.shape[0])

    out_ref[...] = move(matrix[...], in_ref[...])


def block_width(width):
    for block in (384, 256, 128):
        if width % block == 0:
            return block
    return width


def reorder(values, where_to):
    count, width = values.shape
    block = block_width(width)
    return pl.pallas_call(
        reorder_kernel,
        grid=(width // block,),
        out_shape=jax.ShapeDtypeStruct((count, width), jnp.float32),
        in_specs=[
            pl.BlockSpec((1, count), lambda j: (0, 0)),
            pl.BlockSpec((count, block), lambda j: (0, j)),
        ],
        out_specs=pl.BlockSpec((count, block), lambda j: (0, j)),
        scratch_shapes=[pltpu.VMEM((count, count), jnp.bfloat16)],
        compiler_params=pltpu.CompilerParams(vmem_limit_bytes=40 * 2**20),
        cost_estimate=pl.CostEstimate(
            flops=4 * count * count * width, bytes_accessed=8 * count * width, transcendentals=0
        ),
        name="reorder",
    )(where_to.reshape(1, count), values)


def place_kernel(to_ref, limit_ref, direct_ref, other_ref, out_ref, matrix):
    block = pl.program_id(0)

    @pl.when(block == 0)
    def _():
        matrix[...] = pick(to_ref[...], matrix.shape[0])

    count = direct_ref.shape[0]
    value = move(matrix[:, :count], direct_ref[...]) + move(matrix[:, count:], other_ref[...])
    column = lax.broadcasted_iota(jnp.int32, value.shape, 1) + block * value.shape[1]
    out_ref[...] = jnp.where(column >= limit_ref[...], value, 0.0)


def place(direct, other, where_to, limits):
    rows = limits.shape[0]
    width = direct.shape[1]
    block = block_width(width)
    return pl.pallas_call(
        place_kernel,
        grid=(width // block,),
        out_shape=jax.ShapeDtypeStruct((rows, width), jnp.float32),
        in_specs=[
            pl.BlockSpec((1, rows), lambda j: (0, 0)),
            pl.BlockSpec((rows, 1), lambda j: (0, 0)),
            pl.BlockSpec((direct.shape[0], block), lambda j: (0, j)),
            pl.BlockSpec((other.shape[0], block), lambda j: (0, j)),
        ],
        out_specs=pl.BlockSpec((rows, block), lambda j: (0, j)),
        scratch_shapes=[pltpu.VMEM((rows, rows), jnp.bfloat16)],
        compiler_params=pltpu.CompilerParams(vmem_limit_bytes=40 * 2**20),
        cost_estimate=pl.CostEstimate(
            flops=4 * rows * rows * width, bytes_accessed=8 * rows * width, transcendentals=0
        ),
        name="place",
    )(where_to.reshape(1, rows), limits.reshape(rows, 1), direct, other)


def exchange_plan(row_map, groups, rows_dev, base):
    me = lax.axis_index("gr")
    other = rows_dev - groups * base
    every = lax.all_to_all(
        jnp.broadcast_to(row_map[None, :], (groups, rows_dev)), "gr", 0, 0, tiled=True
    )
    dest, slot = every // rows_dev, every % rows_dev
    at = jnp.arange(rows_dev, dtype=jnp.int32)
    before = (at[:, None] < at[None, :]).astype(jnp.bfloat16)
    group_ids = jnp.arange(groups, dtype=jnp.int32)
    onehot = dest[:, None, :] == group_ids[None, :, None]
    ahead = dot(
        onehot.reshape(groups * groups, rows_dev).astype(jnp.bfloat16), before, ((1,), (0,)), None
    ).reshape(groups, groups, rows_dev)
    rank = jnp.sum(jnp.where(onehot, ahead, 0.0), axis=1).astype(jnp.int32)
    late = rank >= base
    late_rank = dot(late.astype(jnp.bfloat16), before, ((1,), (0,)), None).astype(jnp.int32)
    sent = jnp.sum(onehot.astype(jnp.int32), axis=2) - base
    earlier = jnp.cumsum(sent, axis=0) - sent
    start = jnp.sum(jnp.where(onehot, earlier[:, :, None], 0), axis=1)
    turn = start + rank - base
    pack_to = jnp.where(late, groups * base + late_rank, dest * base + rank)
    pack_to = lax.dynamic_index_in_dim(pack_to, me, 0, keepdims=False)
    late_ids = jnp.arange(other, dtype=jnp.int32)
    chosen = late[:, None, :] & (late_rank[:, None, :] == late_ids[None, :, None])
    turn_to = jnp.sum(jnp.where(chosen, (dest * other + turn)[:, None, :], 0), axis=2).reshape(-1)
    arrival = jnp.where(late, groups * base + turn, group_ids[:, None] * base + rank)
    arrival = jnp.where(dest == me, arrival, -1).reshape(-1)
    place_to = jnp.sum(
        jnp.where(arrival[None, :] == at[:, None], slot.reshape(-1)[None, :], 0), axis=1
    )
    return pack_to, turn_to, place_to


def exchange_rows(values, row_map, limits):
    groups = lax.axis_size("gr")
    rows_dev, width = values.shape
    base = 3 * rows_dev // (4 * groups)
    other = rows_dev - groups * base
    part = width // groups
    pack_to, turn_to, place_to = exchange_plan(row_map, groups, rows_dev, base)
    packed = reorder(values, pack_to)
    direct = lax.all_to_all(
        packed[: groups * base].reshape(groups, base, width), "gr", 0, 0, tiled=True
    ).reshape(groups * base, width)
    split = packed[groups * base :].reshape(other, groups, part).transpose(1, 0, 2)
    split = lax.all_to_all(split, "gr", 0, 0, tiled=True).reshape(groups * other, part)
    split = reorder(split, turn_to).reshape(groups, other, part)
    split = lax.all_to_all(split, "gr", 0, 0, tiled=True)
    joined = split.transpose(1, 0, 2).reshape(other, width)
    return place(direct, joined, place_to, limits)


def bits_of(groups):
    count = groups.bit_length() - 1
    orders = (list(range(1, count)), list(range(count - 1, 0, -1)))
    me = lax.axis_index("gr")
    stages = []
    for one, two in zip(*orders):
        pairs = [(i, i ^ (1 << (two if i & 1 else one))) for i in range(groups)]
        mine = jnp.where(me & 1, (me >> two) & 1, (me >> one) & 1)
        stages.append((pairs, mine))
    return stages


def in_plane(pairs, planes, chosen):
    return [(a * planes + z, b * planes + z) for a, b in pairs for z in chosen]


def swap(value, groups):
    return lax.ppermute(value, "gr", [(i, i ^ 1) for i in range(groups)])


def reduce_parts(value, groups, planes, chosen):
    for pairs, mine in bits_of(groups):
        half = value.shape[0] // 2
        keep = lax.dynamic_slice_in_dim(value, mine * half, half, 0)
        give = lax.dynamic_slice_in_dim(value, (1 - mine) * half, half, 0)
        value = keep + lax.ppermute(give, ("gr", "gc"), in_plane(pairs, planes, chosen))
    return value


def join(value, came, mine):
    return jnp.where(
        mine == 0, jnp.concatenate([value, came], axis=0), jnp.concatenate([came, value], axis=0)
    )


def gather_parts(value, groups):
    for pairs, mine in reversed(bits_of(groups)):
        value = join(value, lax.ppermute(value, "gr", pairs), mine)
    return join(value, swap(value, groups), lax.axis_index("gr") & 1)


def from_first_plane(value, planes):
    me = lax.axis_index("gc")
    step = planes // 2
    while step:
        pairs = [(i, i + step) for i in range(0, planes, 2 * step)]
        came = lax.ppermute(value, "gc", pairs)
        value = jnp.where(me % (2 * step) == step, came, value)
        step //= 2
    return value


def shards(child_rows, row_map, stair):
    groups, planes = lax.axis_size("gr"), lax.axis_size("gc")
    me, plane = lax.axis_index("gr"), lax.axis_index("gc")
    core = me & 1
    rows_dev, cols_dev = child_rows.shape
    panels = NPANEL * PANEL
    half = cols_dev // 2
    columns = jnp.arange(cols_dev, dtype=jnp.int32)
    blocks = jnp.arange(stair.shape[0], dtype=jnp.int32)
    child_limits = jnp.sum(
        jnp.where((row_map // STAIR_BLOCK)[:, None] == blocks[None, :], stair[None, :], 0), axis=1
    )
    child_limits = child_limits - plane * cols_dev
    own_blocks = rows_dev // STAIR_BLOCK
    limits = jnp.repeat(
        lax.dynamic_slice_in_dim(stair, me * own_blocks, own_blocks, 0), STAIR_BLOCK
    )
    limits = limits - plane * cols_dev

    masked = jnp.where(columns[None, :] >= child_limits[:, None], child_rows, 0.0)
    panel = masked[:, :panels]
    both = jnp.concatenate([panel, swap(panel, groups)], axis=0)

    share = lax.dynamic_slice_in_dim(both, core * (panels // 2), panels // 2, 1)
    gram = dot(share, both, ((0,), (0,)), HIGHEST)
    gram = reduce_parts(gram, groups, planes, [0])
    gram = from_first_plane(gram, planes)
    gram = gather_parts(gram, groups)
    inverse = inverse_factor(gram)

    panel = from_first_plane(panel, planes)
    both = jnp.concatenate([panel, swap(panel, groups)], axis=0)
    mine = lax.dynamic_slice_in_dim(masked, core * half, half, 1)
    theirs = lax.dynamic_slice_in_dim(masked, (1 - core) * half, half, 1)
    share = jnp.concatenate([mine, swap(theirs, groups)], axis=0)
    product = dot(share, both, ((0,), (0,)), HIGH)
    product = reduce_parts(product, groups, planes, range(planes))
    coupling = dot(product, inverse, ((1,), (1,)), HIGHEST)
    coupling = gather_parts(coupling, groups)

    front = exchange_rows(child_rows, row_map, limits)
    own_panel = from_first_plane(front[:, :panels], planes)
    basis = dot(own_panel, inverse, ((1,), (1,)), HIGHEST)
    projected = front - dot(basis, coupling, ((1,), (1,)), HIGH)
    share_rows = panels // groups
    factor = lax.dynamic_slice_in_dim(coupling, me * share_rows, share_rows, 1).T
    return (factor, projected)


def solution(mesh):
    placed = (P("gr", "gc"), P("gr"), P())
    return jax.shard_map(
        shards,
        mesh=mesh,
        in_specs=placed,
        out_specs=(P("gr", "gc"), P("gr", "gc")),
        check_vma=False,
    )
```

```python
import functools

import jax
import jax.numpy as jnp
from jax import lax
from jax.experimental import pallas as pl
from jax.experimental.pallas import tpu as pltpu
from jax.sharding import PartitionSpec as P

PANEL = 512
NPANEL = 2
STAIR_BLOCK = 128
EDGE = 128
HIGHEST = lax.Precision.HIGHEST
HIGH = lax.Precision.HIGH


def dot(left, right, dims, precision):
    return lax.dot_general(
        left, right, (dims, ((), ())), precision=precision, preferred_element_type=jnp.float32
    )


def split(value):
    high = value.astype(jnp.bfloat16)
    return high, (value - high.astype(jnp.float32)).astype(jnp.bfloat16)


def triple(left, right, dims):
    small = dot(left[0], right[1], dims, None) + dot(left[1], right[0], dims, None)
    return small + dot(left[0], right[0], dims, None)


def eliminate(tiles):
    lane = lax.broadcasted_iota(jnp.int32, (8, EDGE), 1)
    sub = lax.broadcasted_iota(jnp.int32, (8, EDGE), 0)
    tiles = list(tiles)
    strips = len(tiles)
    for strip in range(strips):
        first = 8 * strip
        own = (lane >= first) & (lane < first + 8)
        mult = {
            t: [jnp.broadcast_to(tiles[t][:, first + s : first + s + 1], (8, EDGE)) for s in range(8)]
            for t in range(strip, strips)
        }
        small = [
            [jnp.broadcast_to(mult[strip][s][t : t + 1, :], (8, EDGE)) for s in range(t + 1)]
            for t in range(8)
        ]
        start = jnp.where(own, jnp.where(lane - first == sub, 1.0, 0.0), tiles[strip])
        rows = [jnp.broadcast_to(start[s : s + 1, :], (8, EDGE)) for s in range(8)]
        inv = [None] * 8
        low = [[None] * 8 for _ in range(8)]
        for s in range(8):
            inv[s] = 1.0 / small[s][s]
            for t in range(s + 1, 8):
                low[t][s] = small[t][s] * inv[s]
                for u in range(s + 1, t + 1):
                    small[t][u] = small[t][u] - low[t][s] * small[u][s]
            for t in range(s + 1, 8):
                rows[t] = rows[t] - low[t][s] * rows[s]
        back = [None] * 8
        for s in range(7, -1, -1):
            value = rows[s] * inv[s]
            for t in range(7, s, -1):
                value = value - low[t][s] * back[t]
            back[s] = value
        out, pivot = rows[7], small[7][7]
        for s in range(6, -1, -1):
            out = jnp.where(sub == s, rows[s], out)
            pivot = jnp.where(sub == s, small[s][s], pivot)
        tiles[strip] = out * lax.rsqrt(pivot)
        for t in range(strip + 1, strips):
            value = jnp.where(own, 0.0, tiles[t])
            for s in range(8):
                value = value - mult[t][s] * back[s]
            tiles[t] = value
    return tiles


def unpack(where_ref, chips, halves, work):
    size = work.shape[0]
    blocks = size // EDGE
    for which, half in enumerate(halves):
        core = where_ref[0] ^ which
        rows = half.shape[0] // chips
        for r in range(chips):
            first = (where_ref[1] ^ r) * rows
            pair = core * (blocks // 4) + first // EDGE
            inside = first % EDGE
            for b in range(blocks + 1):
                lead = b <= pair
                row = jnp.where(lead, pair, blocks - 1 - pair)
                col = jnp.where(lead, b, b - pair - 1)
                work[
                    pl.ds(pl.multiple_of(row * EDGE + inside, 8), rows),
                    pl.ds(pl.multiple_of(col * EDGE, EDGE), EDGE),
                ] = half[r * rows : (r + 1) * rows, b * EDGE : (b + 1) * EDGE]
    for i in range(blocks):
        for j in range(i):
            work[j * EDGE : (j + 1) * EDGE, i * EDGE : (i + 1) * EDGE] = work[
                i * EDGE : (i + 1) * EDGE, j * EDGE : (j + 1) * EDGE
            ].T


def inverse_factor_kernel(first, last, chips, *refs):
    out_ref, work, high, low = refs[-4:]
    size = work.shape[0]
    blocks = size // EDGE
    if first == 0:
        unpack(refs[0], chips, refs[1:-4], work)
    else:
        work[...] = refs[0][...]
    lower = lax.broadcasted_iota(jnp.int32, (EDGE, EDGE), 0) >= lax.broadcasted_iota(
        jnp.int32, (EDGE, EDGE), 1
    )

    @pl.loop(first, last)
    def _(k):
        at = pl.multiple_of(k * EDGE, EDGE)
        tiles = [
            work[pl.ds(pl.multiple_of(at + 8 * t, 8), 8), pl.ds(at, EDGE)] for t in range(EDGE // 8)
        ]
        diag = jnp.where(lower, jnp.concatenate(eliminate(tiles), axis=0), 0.0)
        work[pl.ds(at, EDGE), :] = triple(split(diag), split(work[pl.ds(at, EDGE), :]), ((1,), (0,)))
        work[pl.ds(at, EDGE), pl.ds(at, EDGE)] = diag
        high[...], low[...] = split(work[pl.ds(at, EDGE), :])

        @pl.loop(k + 1, blocks)
        def _(i):
            below = pl.multiple_of(i * EDGE, EDGE)
            coeff = high[:, pl.ds(below, EDGE)], low[:, pl.ds(below, EDGE)]
            work[pl.ds(below, EDGE), pl.ds(at, EDGE)] = jnp.zeros((EDGE, EDGE), jnp.float32)
            work[pl.ds(below, EDGE), :] -= triple(coeff, (high[...], low[...]), ((0,), (0,)))

    if last == blocks:
        for k in range(blocks - 1):
            work[k * EDGE : (k + 1) * EDGE, (k + 1) * EDGE :] = jnp.zeros(
                (EDGE, size - (k + 1) * EDGE), jnp.float32
            )
    out_ref[...] = work[...]


def inverse_factor(held, size, first, last, chips):
    vmem = pl.BlockSpec(memory_space=pltpu.VMEM)
    specs = [vmem] if first else [pl.BlockSpec(memory_space=pltpu.SMEM), vmem, vmem]
    return pl.pallas_call(
        functools.partial(inverse_factor_kernel, first, last, chips),
        out_shape=jax.ShapeDtypeStruct((size, size), jnp.float32),
        in_specs=specs,
        out_specs=vmem,
        scratch_shapes=[pltpu.VMEM((size, size), jnp.float32)]
        + [pltpu.VMEM((EDGE, size), jnp.bfloat16)] * 2,
        compiler_params=pltpu.CompilerParams(vmem_limit_bytes=40 * 2**20),
        cost_estimate=pl.CostEstimate(
            flops=4 * 2 * size**3, bytes_accessed=32 * size * size, transcendentals=size
        ),
        name="inverse_factor",
    )(*held)


def pick(where_to, count):
    rows = lax.broadcasted_iota(jnp.int32, (count, where_to.shape[1]), 0)
    return jnp.where(rows == where_to, 1.0, 0.0).astype(jnp.bfloat16)


def move(matrix, values):
    high = values.astype(jnp.bfloat16)
    rest = (values - high.astype(jnp.float32)).astype(jnp.bfloat16)
    dims = ((1,), (0,))
    return dot(matrix, high, dims, None) + dot(matrix, rest, dims, None)


def reorder_kernel(to_ref, in_ref, out_ref, matrix):
    matrix[...] = pick(to_ref[...], matrix.shape[0])
    out_ref[...] = move(matrix[...], in_ref[...])


def reorder(values, where_to):
    count, width = values.shape
    return pl.pallas_call(
        reorder_kernel,
        out_shape=jax.ShapeDtypeStruct((count, width), jnp.float32),
        in_specs=[pl.BlockSpec(memory_space=pltpu.VMEM)] * 2,
        out_specs=pl.BlockSpec(memory_space=pltpu.VMEM),
        scratch_shapes=[pltpu.VMEM((count, count), jnp.bfloat16)],
        compiler_params=pltpu.CompilerParams(vmem_limit_bytes=40 * 2**20),
        cost_estimate=pl.CostEstimate(
            flops=4 * count * count * width, bytes_accessed=8 * count * width, transcendentals=0
        ),
        name="reorder",
    )(where_to.reshape(1, count), values)


def block_width(width):
    for block in (512, 384, 256, 128):
        if width % block == 0:
            return block
    return width


def pack_kernel(to_ref, in_ref, direct_ref, other_ref, matrix):
    @pl.when(pl.program_id(0) == 0)
    def _():
        matrix[...] = pick(to_ref[...], matrix.shape[0])

    count = direct_ref.shape[0]
    value = move(matrix[...], in_ref[...])
    direct_ref[...] = value[:count]
    other_ref[...] = value[count:]


def pack(values, where_to, count):
    rows, width = values.shape
    block = block_width(width)
    return pl.pallas_call(
        pack_kernel,
        grid=(width // block,),
        out_shape=[
            jax.ShapeDtypeStruct((count, width), jnp.float32),
            jax.ShapeDtypeStruct((rows - count, width), jnp.float32),
        ],
        in_specs=[
            pl.BlockSpec((1, rows), lambda j: (0, 0)),
            pl.BlockSpec((rows, block), lambda j: (0, j)),
        ],
        out_specs=[
            pl.BlockSpec((count, block), lambda j: (0, j)),
            pl.BlockSpec((rows - count, block), lambda j: (0, j)),
        ],
        scratch_shapes=[pltpu.VMEM((rows, rows), jnp.bfloat16)],
        compiler_params=pltpu.CompilerParams(vmem_limit_bytes=40 * 2**20),
        cost_estimate=pl.CostEstimate(
            flops=4 * rows * rows * width, bytes_accessed=8 * rows * width, transcendentals=0
        ),
        name="pack",
    )(where_to.reshape(1, rows), values)


def place_kernel(offset, to_ref, limit_ref, direct_ref, other_ref, *rest):
    out_ref, matrix = rest[-2:]
    block = pl.program_id(0)

    @pl.when(block == 0)
    def _():
        matrix[...] = pick(to_ref[...], matrix.shape[0])

    count = direct_ref.shape[0]
    value = move(matrix[:, :count], direct_ref[...]) + move(matrix[:, count:], other_ref[...])
    column = lax.broadcasted_iota(jnp.int32, value.shape, 1) + (block + offset) * value.shape[1]
    out_ref[...] = jnp.where(column >= limit_ref[...], value, 0.0)


def place(direct, other, where_to, limits, front, start):
    rows = limits.shape[0]
    width, full = direct.shape[1], other.shape[1]
    block = block_width(width)
    offset = start // block
    held = [] if front is None else [front]
    return pl.pallas_call(
        functools.partial(place_kernel, offset),
        grid=(width // block,),
        out_shape=jax.ShapeDtypeStruct((rows, full), jnp.float32),
        in_specs=[
            pl.BlockSpec((1, rows), lambda j: (0, 0)),
            pl.BlockSpec((rows, 1), lambda j: (0, 0)),
            pl.BlockSpec((direct.shape[0], block), lambda j: (0, j)),
            pl.BlockSpec((other.shape[0], block), lambda j: (0, j + offset)),
        ]
        + [pl.BlockSpec(memory_space=pl.ANY) for _ in held],
        out_specs=pl.BlockSpec((rows, block), lambda j: (0, j + offset)),
        scratch_shapes=[pltpu.VMEM((rows, rows), jnp.bfloat16)],
        input_output_aliases={4: 0} if held else {},
        compiler_params=pltpu.CompilerParams(vmem_limit_bytes=40 * 2**20),
        cost_estimate=pl.CostEstimate(
            flops=4 * rows * rows * width, bytes_accessed=8 * rows * width, transcendentals=0
        ),
        name="place",
    )(where_to.reshape(1, rows), limits.reshape(rows, 1), direct, other, *held)


def basis_kernel(panel_ref, inverse_ref, high_ref, low_ref):
    value = triple(split(panel_ref[...]), split(inverse_ref[...]), ((1,), (1,)))
    high_ref[...], low_ref[...] = split(value)


def basis_of(panel, inverse):
    rows, panels = panel.shape
    vmem = pl.BlockSpec(memory_space=pltpu.VMEM)
    return pl.pallas_call(
        basis_kernel,
        out_shape=[jax.ShapeDtypeStruct((rows, panels), jnp.bfloat16)] * 2,
        in_specs=[vmem] * 2,
        out_specs=[vmem] * 2,
        compiler_params=pltpu.CompilerParams(vmem_limit_bytes=56 * 2**20),
        cost_estimate=pl.CostEstimate(
            flops=6 * rows * panels * panels,
            bytes_accessed=4 * panels * (2 * rows + panels),
            transcendentals=0,
        ),
        name="basis",
    )(panel, inverse)


def project_kernel(count, where_ref, high_ref, low_ref, front_ref, *rest):
    pieces, rest = rest[:count], rest[count:]
    shares, rest = rest[:count], rest[count:]
    out_ref, factor_ref, one, two = rest[-4:]
    step, part = pl.program_id(0), pl.program_id(1)
    rows = out_ref.shape[0]
    for i in range(count):

        @pl.when((step == i) & (part == 0))
        def _():
            one[...], two[...] = split(pieces[i][...])
            factor_ref[...] = shares[i][...]

    own = pl.ds(pl.multiple_of(part * rows, rows), rows)
    basis = high_ref[own, :], low_ref[own, :]
    out_ref[...] = front_ref[...] - triple(basis, (one[...], two[...]), ((1,), (0,)))


def project(front, factor, basis, pieces, where, me):
    rows, full = front.shape
    panels, width = pieces[0].shape
    count = len(pieces)
    share = panels // lax.axis_size("gr")
    place_at = jnp.stack(list(where) + [me]).astype(jnp.int32)
    held = [] if factor is None else [factor]
    whole = pl.BlockSpec((rows, panels), lambda j, k, at: (0, 0))
    block = pl.BlockSpec((rows // 2, width), lambda j, k, at: (k, at[j]))
    return pl.pallas_call(
        functools.partial(project_kernel, count),
        grid_spec=pltpu.PrefetchScalarGridSpec(
            num_scalar_prefetch=1,
            grid=(count, 2),
            in_specs=[whole, whole, block]
            + [pl.BlockSpec((panels, width), lambda j, k, at: (0, 0)) for _ in pieces]
            + [pl.BlockSpec((share, width), lambda j, k, at: (at[count], 0)) for _ in pieces]
            + [pl.BlockSpec(memory_space=pl.ANY) for _ in held],
            out_specs=[block, pl.BlockSpec((share, width), lambda j, k, at: (0, at[j]))],
            scratch_shapes=[pltpu.VMEM((panels, width), jnp.bfloat16)] * 2,
        ),
        out_shape=[
            jax.ShapeDtypeStruct((rows, full), jnp.float32),
            jax.ShapeDtypeStruct((share, full), jnp.float32),
        ],
        input_output_aliases={3: 0, 4 + 2 * count: 1} if held else {3: 0},
        compiler_params=pltpu.CompilerParams(vmem_limit_bytes=56 * 2**20),
        cost_estimate=pl.CostEstimate(
            flops=6 * rows * panels * width * count,
            bytes_accessed=4 * count * (2 * rows + panels) * width,
            transcendentals=0,
        ),
        name="project",
    )(place_at, *basis, front, *pieces, *pieces, *held)


def pack_plan(row_map, groups, rows_dev, base):
    dest = row_map // rows_dev
    at = jnp.arange(rows_dev, dtype=jnp.int32)
    before = (at[:, None] < at[None, :]).astype(jnp.bfloat16)
    onehot = dest[None, :] == jnp.arange(groups, dtype=jnp.int32)[:, None]
    ahead = dot(onehot.astype(jnp.bfloat16), before, ((1,), (0,)), None)
    rank = jnp.sum(jnp.where(onehot, ahead, 0.0), axis=0).astype(jnp.int32)
    late = rank >= base
    late_rank = dot(late[None, :].astype(jnp.bfloat16), before, ((1,), (0,)), None)[0]
    return jnp.where(late, groups * base + late_rank.astype(jnp.int32), dest * base + rank)


def arrival_plan(every, rows_dev, base):
    me = lax.axis_index("gr")
    groups = every.shape[0]
    other = rows_dev - groups * base
    dest, slot = every // rows_dev, every % rows_dev
    at = jnp.arange(rows_dev, dtype=jnp.int32)
    before = (at[:, None] < at[None, :]).astype(jnp.bfloat16)
    group_ids = jnp.arange(groups, dtype=jnp.int32)
    onehot = dest[:, None, :] == group_ids[None, :, None]
    ahead = dot(
        onehot.reshape(groups * groups, rows_dev).astype(jnp.bfloat16), before, ((1,), (0,)), None
    ).reshape(groups, groups, rows_dev)
    rank = jnp.sum(jnp.where(onehot, ahead, 0.0), axis=1).astype(jnp.int32)
    late = rank >= base
    late_rank = dot(late.astype(jnp.bfloat16), before, ((1,), (0,)), None).astype(jnp.int32)
    sent = jnp.sum(onehot.astype(jnp.int32), axis=2) - base
    earlier = jnp.cumsum(sent, axis=0) - sent
    start = jnp.sum(jnp.where(onehot, earlier[:, :, None], 0), axis=1)
    turn = start + rank - base
    late_ids = jnp.arange(other, dtype=jnp.int32)
    chosen = late[:, None, :] & (late_rank[:, None, :] == late_ids[None, :, None])
    turn_to = jnp.sum(jnp.where(chosen, (dest * other + turn)[:, None, :], 0), axis=2).reshape(-1)
    arrival = jnp.where(late, groups * base + turn, group_ids[:, None] * base + rank)
    arrival = jnp.where(dest == me, arrival, -1).reshape(-1)
    place_to = jnp.sum(
        jnp.where(arrival[None, :] == at[:, None], slot.reshape(-1)[None, :], 0), axis=1
    )
    return turn_to, place_to


def to_all(value):
    return lax.all_to_all(value, "gr", 0, 0, tiled=True)


def turn_rows(spread, turn_to):
    groups, other, part = spread.shape
    return reorder(spread.reshape(groups * other, part), turn_to).reshape(groups, other, part)


def after(value, *others):
    if isinstance(value, (list, tuple)):
        return list(lax.optimization_barrier(tuple(value) + others)[: len(value)])
    return lax.optimization_barrier((value,) + others)[0]


def stages_of(groups, core):
    count = groups.bit_length() - 1
    me = lax.axis_index("gr")
    found = []
    for one, two in zip(range(1, count), range(count - 1, 0, -1)):
        pairs = [(i, i ^ (1 << (two if i & 1 else one))) for i in range(groups)]
        found.append((pairs, jnp.where(core == 1, (me >> two) & 1, (me >> one) & 1)))
    return found


def swap(value):
    groups = lax.axis_size("gr")
    return lax.ppermute(value, "gr", [(i, i ^ 1) for i in range(groups)])


def position(index, stages, core):
    at = core
    for j, (_, mine) in enumerate(stages):
        at = 2 * at + (mine ^ ((index >> (len(stages) - 1 - j)) & 1))
    return at


def chip_pairs(r, planes, chosen):
    groups = lax.axis_size("gr")
    return [
        (i * planes + z, (i ^ (2 * r)) * planes + z) for i in range(groups) for z in chosen
    ]


def reduce_direct(value, planes, chosen):
    chips = lax.axis_size("gr") // 2
    chip = lax.axis_index("gr") // 2
    size = value.shape[0] // chips

    def rows_of(r):
        return lax.dynamic_slice_in_dim(value, (chip ^ r) * size, size, 0)

    came = [
        lax.ppermute(rows_of(r), ("gr", "gc"), chip_pairs(r, planes, chosen))
        for r in range(chips - 1, 0, -1)
    ]
    total = rows_of(0)
    for one in came:
        total = total + one
    return total


def gather_direct(value, planes, wait):
    chips = lax.axis_size("gr") // 2
    every = range(planes)
    came = [
        lax.ppermute(value, ("gr", "gc"), chip_pairs(r, planes, every)) for r in range(1, chips)
    ]
    came = after(came, wait)
    return jnp.concatenate([value] + came, axis=0)


def send_stage(pieces, j):
    groups = lax.axis_size("gr")
    stages = stages_of(groups, lax.axis_index("gr") & 1)
    bit = 1 << (len(stages) - 1 - j)
    order = sorted((i for i in pieces if i & bit), reverse=True)
    came = [lax.ppermute(pieces[i], "gr", stages[j][0]) for i in order]
    return {i ^ bit: pieces[i ^ bit] for i in order}, came


def add_stage(left, came):
    return {i: left[i] + one for i, one in zip(left, came)}


def pieces_of(value):
    stages = stages_of(lax.axis_size("gr"), lax.axis_index("gr") & 1)
    size = value.shape[0] >> len(stages)
    return {
        i: lax.dynamic_slice_in_dim(value, position(i, stages, jnp.int32(0)) * size, size, 0)
        for i in range(1 << len(stages))
    }


def gather_pieces(piece, use):
    core = lax.axis_index("gr") & 1
    stages, others = stages_of(lax.axis_size("gr"), core), stages_of(lax.axis_size("gr"), 1 - core)
    pieces = {0: piece}

    def take(i):
        return use(
            [pieces[i], swap(pieces[i])],
            [position(i, stages, core), position(i, others, 1 - core)],
        )

    for j in range(len(stages) - 1, -1, -1):
        bit = 1 << (len(stages) - 1 - j)
        pieces[bit] = lax.ppermute(piece, "gr", stages[j][0])
    done = take(0)
    for i in pieces:
        pieces[i] = after(pieces[i], done)
    for j in range(len(stages) - 2, -1, -1):
        bit = 1 << (len(stages) - 1 - j)
        for i in range(1, bit):
            pieces[i | bit] = lax.ppermute(pieces[i], "gr", stages[j][0])
    for i in sorted(i for i in pieces if i):
        pieces[i] = after(pieces[i], done) if i == len(pieces) - 1 else pieces[i]
        done = take(i)


def to_planes(value, planes):
    if planes > 4:
        return [tree_from_first_plane(value, planes)]
    return [lax.ppermute(value, "gc", [(0, i)]) for i in range(1, planes)]


def from_first_plane(value, came, planes):
    me = lax.axis_index("gc")
    if planes > 4:
        return came[0]
    for i in range(1, planes):
        value = jnp.where(me == i, came[i - 1], value)
    return value


def tree_from_first_plane(value, planes):
    me = lax.axis_index("gc")
    step = planes // 2
    while step:
        pairs = [(i, i + step) for i in range(0, planes, 2 * step)]
        came = lax.ppermute(value, "gc", pairs)
        value = jnp.where(me % (2 * step) == step, came, value)
        step //= 2
    return value


def thirds_of(value):
    rows = value.shape[0]
    size = -(-rows // 24) * 8
    return [lax.slice_in_dim(value, s, s + size) for s in (0, rows - 2 * size, rows - size)]


def send_thirds(value, planes):
    if planes != 4:
        return [tree_from_first_plane(value, planes)]
    return [lax.ppermute(part, "gc", [(0, i + 1)]) for i, part in enumerate(thirds_of(value))]


def join_thirds(value, came, planes, wait):
    if planes != 4:
        return came[0]
    me = lax.axis_index("gc")
    own = jnp.where(me == 1, came[0], jnp.where(me == 2, came[1], came[2]))
    thirds = thirds_of(value)
    one = lax.ppermute(own, "gc", [(1, 2), (2, 3), (3, 1)])
    two = lax.ppermute(own, "gc", [(1, 3), (2, 1), (3, 2)])
    one, two = after([one, two], *wait)
    found = []
    for i in range(3):
        held = [own, one, two] if i == 0 else ([two, own, one] if i == 1 else [one, two, own])
        part = jnp.where(me == 1, held[0], jnp.where(me == 2, held[1], held[2]))
        found.append(jnp.where(me == 0, thirds[i], part))
    found[0] = found[0][: value.shape[0] - 2 * own.shape[0]]
    return jnp.concatenate(found, axis=0)


def shards(child_rows, row_map, stair):
    groups, planes = lax.axis_size("gr"), lax.axis_size("gc")
    me, plane = lax.axis_index("gr"), lax.axis_index("gc")
    core = me & 1
    rows_dev, cols_dev = child_rows.shape
    panels = NPANEL * PANEL
    half = cols_dev // 2
    blocks = panels // EDGE
    base = 3 * rows_dev // (4 * groups)
    columns = jnp.arange(cols_dev, dtype=jnp.int32)
    stair_ids = jnp.arange(stair.shape[0], dtype=jnp.int32)
    child_limits = jnp.sum(
        jnp.where((row_map // STAIR_BLOCK)[:, None] == stair_ids[None, :], stair[None, :], 0), axis=1
    )
    child_limits = child_limits - plane * cols_dev
    own_blocks = rows_dev // STAIR_BLOCK
    limits = jnp.repeat(
        lax.dynamic_slice_in_dim(stair, me * own_blocks, own_blocks, 0), STAIR_BLOCK
    )
    limits = limits - plane * cols_dev
    everyone = range(planes)

    panel = jnp.where(columns[None, :panels] >= child_limits[:, None], child_rows[:, :panels], 0.0)
    both = jnp.concatenate([panel, swap(panel)], axis=0)

    panel_came = send_thirds(panel, planes)

    quarter = panels // 4
    outer = jnp.concatenate([both[:, :quarter], both[:, 3 * quarter :]], axis=1)
    share = jnp.where(core == 0, outer, both[:, quarter : 3 * quarter])
    gram = dot(share, both, ((0,), (0,)), HIGHEST)
    packed = []
    for lead in (0, blocks // 4):
        rows = []
        for i in range(blocks // 4):
            one, two = lead + i + 1, blocks - lead - i
            last = blocks // 2 - 1 - i
            rows.append(
                jnp.concatenate(
                    [
                        gram[i * EDGE : (i + 1) * EDGE, : one * EDGE],
                        gram[last * EDGE : (last + 1) * EDGE, : two * EDGE],
                    ],
                    axis=1,
                )
            )
        packed.append(jnp.concatenate(rows, axis=0))
    gram = jnp.where(core == 0, packed[0], packed[1])
    gram_sum = reduce_direct(gram, planes, [0])
    count = groups * base
    every = to_all(after(jnp.broadcast_to(row_map[None, :], (groups, rows_dev)), gram))
    pack_to = pack_plan(row_map, groups, rows_dev, base)
    direct, spread = pack(child_rows, after(pack_to, gram), count)
    spread = to_all(spread.reshape(rows_dev - count, groups, -1).transpose(1, 0, 2))
    panel_came = after(panel_came, gram_sum)
    gram_came = to_planes(gram_sum, planes)

    spread = after(spread, gram_sum)
    width = panels if cols_dev % panels == 0 else cols_dev
    first = after(direct[:, :width], spread)
    first = to_all(first.reshape(groups, base, width)).reshape(count, width)
    turn_to, place_to = arrival_plan(every, rows_dev, base)
    turn_to, place_to = lax.optimization_barrier((turn_to, place_to))
    spread = turn_rows(spread, turn_to)

    halves = []
    child = after(child_rows, gram_sum)
    for start in (core * half, (1 - core) * half):
        value = lax.dynamic_slice_in_dim(child, start, half, 1)
        halves.append(jnp.where(start + columns[None, :half] >= child_limits[:, None], value, 0.0))
    share = jnp.concatenate([halves[0], swap(halves[1])], axis=0)
    gram_came = after(gram_came, spread, halves[0], halves[1])
    gram_first = from_first_plane(gram_sum, gram_came, planes)
    everywhere = join_thirds(panel, panel_came, planes, (gram_first, first))
    spread = to_all(after(spread, first, gram_first))
    both = jnp.concatenate([everywhere, swap(everywhere)], axis=0)
    product = dot(share, after(both, gram_first), ((0,), (0,)), HIGH)
    gram = gather_direct(gram_first, planes, product)
    grams = [jnp.stack([core, me // 2]).astype(jnp.int32), gram, swap(gram)]
    product, came = send_stage(pieces_of(after(product, gram)), 0)

    spread = after(spread, *product.values())
    spread = spread.transpose(1, 0, 2).reshape(rows_dev - count, cols_dev)
    front = place(first, spread, place_to, limits, None, 0)
    if width < cols_dev:
        second = after(direct[:, width:], spread)
        second = to_all(second.reshape(groups, base, -1)).reshape(count, -1)
    own_panel = front[:, :panels]
    own_came = send_thirds(own_panel, planes)
    grams = after(grams, front)

    inverse = inverse_factor(grams, panels, 0, blocks // 2, groups // 2)
    came = after(came, inverse)
    product = add_stage(product, came)
    own_came = after(own_came, *product.values())
    own_panel = join_thirds(own_panel, own_came, planes, (inverse,))
    for j in range(1, groups.bit_length() - 2):
        product, came = send_stage(product, j)
        last = j == groups.bit_length() - 3
        if last:
            inverse = inverse_factor(
                [after(inverse, *own_came, *product.values())], panels, blocks // 2, blocks, groups // 2
            )
            came = after(came, inverse)
        product = add_stage(product, came)
    product = product[0]
    coupling = dot(inverse, product, ((1,), (1,)), HIGH)
    basis = basis_of(own_panel, inverse)
    if width < cols_dev:
        front = place(second, spread, after(place_to, coupling), limits, front, width)
    piece_cols = coupling.shape[1]
    if piece_cols % EDGE == 0:
        held = [front, None]

        def use(pieces, where):
            held[:] = project(held[0], held[1], basis, pieces, where, me)
            return held[1]

        gather_pieces(coupling, use)
        return (held[1], held[0])
    held = [jnp.zeros((panels, cols_dev), jnp.float32)]

    def keep(pieces, where):
        for piece, at in zip(pieces, where):
            held[0] = lax.dynamic_update_slice_in_dim(held[0], piece, at * piece_cols, 1)
        return pieces[0]

    gather_pieces(coupling, keep)
    whole = held[0]
    share_rows = panels // groups
    factor = lax.dynamic_slice_in_dim(whole, me * share_rows, share_rows, 0)
    basis = basis[0].astype(jnp.float32) + basis[1].astype(jnp.float32)
    return (factor, front - dot(basis, whole, ((1,), (0,)), HIGH))


def solution(mesh):
    placed = (P("gr", "gc"), P("gr"), P())
    return jax.shard_map(
        shards,
        mesh=mesh,
        in_specs=placed,
        out_specs=(P("gr", "gc"), P("gr", "gc")),
        check_vma=False,
    )
```

```python
import functools

import jax
import jax.numpy as jnp
from jax import lax
from jax.experimental import pallas as pl
from jax.experimental.pallas import tpu as pltpu
from jax.sharding import PartitionSpec as P

PANEL = 512
NPANEL = 2
STAIR_BLOCK = 128
EDGE = 128
HIGHEST = lax.Precision.HIGHEST
HIGH = lax.Precision.HIGH


def dot(left, right, dims, precision):
    return lax.dot_general(
        left, right, (dims, ((), ())), precision=precision, preferred_element_type=jnp.float32
    )


def split(value):
    high = value.astype(jnp.bfloat16)
    return high, (value - high.astype(jnp.float32)).astype(jnp.bfloat16)


def triple(left, right, dims):
    small = dot(left[0], right[1], dims, None) + dot(left[1], right[0], dims, None)
    return small + dot(left[0], right[0], dims, None)


def eliminate(tiles):
    lane = lax.broadcasted_iota(jnp.int32, (8, EDGE), 1)
    sub = lax.broadcasted_iota(jnp.int32, (8, EDGE), 0)
    tiles = list(tiles)
    strips = len(tiles)
    for strip in range(strips):
        first = 8 * strip
        own = (lane >= first) & (lane < first + 8)
        mult = {
            t: [jnp.broadcast_to(tiles[t][:, first + s : first + s + 1], (8, EDGE)) for s in range(8)]
            for t in range(strip, strips)
        }
        small = [
            [jnp.broadcast_to(mult[strip][s][t : t + 1, :], (8, EDGE)) for s in range(t + 1)]
            for t in range(8)
        ]
        start = jnp.where(own, jnp.where(lane - first == sub, 1.0, 0.0), tiles[strip])
        rows = [jnp.broadcast_to(start[s : s + 1, :], (8, EDGE)) for s in range(8)]
        inv = [None] * 8
        low = [[None] * 8 for _ in range(8)]
        for s in range(8):
            inv[s] = 1.0 / small[s][s]
            for t in range(s + 1, 8):
                low[t][s] = small[t][s] * inv[s]
                for u in range(s + 1, t + 1):
                    small[t][u] = small[t][u] - low[t][s] * small[u][s]
            for t in range(s + 1, 8):
                rows[t] = rows[t] - low[t][s] * rows[s]
        back = [None] * 8
        for s in range(7, -1, -1):
            value = rows[s] * inv[s]
            for t in range(7, s, -1):
                value = value - low[t][s] * back[t]
            back[s] = value
        out, pivot = rows[7], small[7][7]
        for s in range(6, -1, -1):
            out = jnp.where(sub == s, rows[s], out)
            pivot = jnp.where(sub == s, small[s][s], pivot)
        tiles[strip] = out * lax.rsqrt(pivot)
        for t in range(strip + 1, strips):
            value = jnp.where(own, 0.0, tiles[t])
            for s in range(8):
                value = value - mult[t][s] * back[s]
            tiles[t] = value
    return tiles


def unpack(where_ref, chips, halves, work):
    size = work.shape[0]
    blocks = size // EDGE
    for which, half in enumerate(halves):
        core = where_ref[0] ^ which
        rows = half.shape[0] // chips
        for r in range(chips):
            first = (where_ref[1] ^ r) * rows
            pair = core * (blocks // 4) + first // EDGE
            inside = first % EDGE
            for b in range(blocks + 1):
                lead = b <= pair
                row = jnp.where(lead, pair, blocks - 1 - pair)
                col = jnp.where(lead, b, b - pair - 1)
                work[
                    pl.ds(pl.multiple_of(row * EDGE + inside, 8), rows),
                    pl.ds(pl.multiple_of(col * EDGE, EDGE), EDGE),
                ] = half[r * rows : (r + 1) * rows, b * EDGE : (b + 1) * EDGE]
    for i in range(blocks):
        for j in range(i):
            work[j * EDGE : (j + 1) * EDGE, i * EDGE : (i + 1) * EDGE] = work[
                i * EDGE : (i + 1) * EDGE, j * EDGE : (j + 1) * EDGE
            ].T


def inverse_factor_kernel(first, last, chips, *refs):
    out_ref, work, high, low = refs[-4:]
    size = work.shape[0]
    blocks = size // EDGE
    if first == 0:
        unpack(refs[0], chips, refs[1:-4], work)
    else:
        work[...] = refs[0][...]
    lower = lax.broadcasted_iota(jnp.int32, (EDGE, EDGE), 0) >= lax.broadcasted_iota(
        jnp.int32, (EDGE, EDGE), 1
    )

    @pl.loop(first, last)
    def _(k):
        at = pl.multiple_of(k * EDGE, EDGE)
        tiles = [
            work[pl.ds(pl.multiple_of(at + 8 * t, 8), 8), pl.ds(at, EDGE)] for t in range(EDGE // 8)
        ]
        diag = jnp.where(lower, jnp.concatenate(eliminate(tiles), axis=0), 0.0)
        work[pl.ds(at, EDGE), :] = triple(split(diag), split(work[pl.ds(at, EDGE), :]), ((1,), (0,)))
        work[pl.ds(at, EDGE), pl.ds(at, EDGE)] = diag
        high[...], low[...] = split(work[pl.ds(at, EDGE), :])

        @pl.loop(k + 1, blocks)
        def _(i):
            below = pl.multiple_of(i * EDGE, EDGE)
            coeff = high[:, pl.ds(below, EDGE)], low[:, pl.ds(below, EDGE)]
            work[pl.ds(below, EDGE), pl.ds(at, EDGE)] = jnp.zeros((EDGE, EDGE), jnp.float32)
            work[pl.ds(below, EDGE), :] -= triple(coeff, (high[...], low[...]), ((0,), (0,)))

    if last == blocks:
        for k in range(blocks - 1):
            work[k * EDGE : (k + 1) * EDGE, (k + 1) * EDGE :] = jnp.zeros(
                (EDGE, size - (k + 1) * EDGE), jnp.float32
            )
    out_ref[...] = work[...]


def inverse_factor(held, size, first, last, chips):
    vmem = pl.BlockSpec(memory_space=pltpu.VMEM)
    specs = [vmem] if first else [pl.BlockSpec(memory_space=pltpu.SMEM), vmem, vmem]
    return pl.pallas_call(
        functools.partial(inverse_factor_kernel, first, last, chips),
        out_shape=jax.ShapeDtypeStruct((size, size), jnp.float32),
        in_specs=specs,
        out_specs=vmem,
        scratch_shapes=[pltpu.VMEM((size, size), jnp.float32)]
        + [pltpu.VMEM((EDGE, size), jnp.bfloat16)] * 2,
        compiler_params=pltpu.CompilerParams(vmem_limit_bytes=40 * 2**20),
        cost_estimate=pl.CostEstimate(
            flops=32 * size**3, bytes_accessed=32 * size * size, transcendentals=size
        ),
        name="inverse_factor",
    )(*held)


def pick(where_to, count):
    rows = lax.broadcasted_iota(jnp.int32, (count, where_to.shape[1]), 0)
    return jnp.where(rows == where_to, 1.0, 0.0).astype(jnp.bfloat16)


def move(matrix, values):
    high = values.astype(jnp.bfloat16)
    rest = (values - high.astype(jnp.float32)).astype(jnp.bfloat16)
    dims = ((1,), (0,))
    return dot(matrix, high, dims, None) + dot(matrix, rest, dims, None)


def reorder_kernel(to_ref, in_ref, out_ref, matrix):
    matrix[...] = pick(to_ref[...], matrix.shape[0])
    out_ref[...] = move(matrix[...], in_ref[...])


def reorder(values, where_to):
    count, width = values.shape
    return pl.pallas_call(
        reorder_kernel,
        out_shape=jax.ShapeDtypeStruct((count, width), jnp.float32),
        in_specs=[pl.BlockSpec(memory_space=pltpu.VMEM)] * 2,
        out_specs=pl.BlockSpec(memory_space=pltpu.VMEM),
        scratch_shapes=[pltpu.VMEM((count, count), jnp.bfloat16)],
        compiler_params=pltpu.CompilerParams(vmem_limit_bytes=40 * 2**20),
        cost_estimate=pl.CostEstimate(
            flops=4 * count * count * width, bytes_accessed=8 * count * width, transcendentals=0
        ),
        name="reorder",
    )(where_to.reshape(1, count), values)


def block_width(width):
    for block in (512, 384, 256, 128):
        if width % block == 0:
            return block
    return width


def pack_kernel(to_ref, in_ref, direct_ref, other_ref, matrix):
    @pl.when(pl.program_id(0) == 0)
    def _():
        matrix[...] = pick(to_ref[...], matrix.shape[0])

    count = direct_ref.shape[0]
    value = move(matrix[...], in_ref[...])
    direct_ref[...] = value[:count]
    other_ref[...] = value[count:]


def pack(values, where_to, count):
    rows, width = values.shape
    block = block_width(width)
    return pl.pallas_call(
        pack_kernel,
        grid=(width // block,),
        out_shape=[
            jax.ShapeDtypeStruct((count, width), jnp.float32),
            jax.ShapeDtypeStruct((rows - count, width), jnp.float32),
        ],
        in_specs=[
            pl.BlockSpec((1, rows), lambda j: (0, 0)),
            pl.BlockSpec((rows, block), lambda j: (0, j)),
        ],
        out_specs=[
            pl.BlockSpec((count, block), lambda j: (0, j)),
            pl.BlockSpec((rows - count, block), lambda j: (0, j)),
        ],
        scratch_shapes=[pltpu.VMEM((rows, rows), jnp.bfloat16)],
        compiler_params=pltpu.CompilerParams(vmem_limit_bytes=40 * 2**20),
        cost_estimate=pl.CostEstimate(
            flops=4 * rows * rows * width, bytes_accessed=8 * rows * width, transcendentals=0
        ),
        name="pack",
    )(where_to.reshape(1, rows), values)


def place_kernel(offset, outs, to_ref, limit_ref, direct_ref, other_ref, *rest):
    out_refs, matrix = rest[len(rest) - 1 - outs : -1], rest[-1]
    block = pl.program_id(0)

    @pl.when(block == 0)
    def _():
        matrix[...] = pick(to_ref[...], matrix.shape[0])

    count = direct_ref.shape[0]
    value = move(matrix[:, :count], direct_ref[...]) + move(matrix[:, count:], other_ref[...])
    column = lax.broadcasted_iota(jnp.int32, value.shape, 1) + (block + offset) * value.shape[1]
    for out_ref in out_refs:
        out_ref[...] = jnp.where(column >= limit_ref[...], value, 0.0)


def place(direct, other, where_to, limits, front, start):
    rows = limits.shape[0]
    width, full = direct.shape[1], other.shape[1]
    block = block_width(width)
    offset = start // block
    held = [] if front is None else [front]
    outs = [jax.ShapeDtypeStruct((rows, full), jnp.float32)]
    out_specs = [pl.BlockSpec((rows, block), lambda j: (0, j + offset))]
    if not held:
        outs.append(jax.ShapeDtypeStruct((rows, width), jnp.float32))
        out_specs.append(pl.BlockSpec((rows, block), lambda j: (0, j)))
    return pl.pallas_call(
        functools.partial(place_kernel, offset, len(outs)),
        grid=(width // block,),
        out_shape=outs,
        in_specs=[
            pl.BlockSpec((1, rows), lambda j: (0, 0)),
            pl.BlockSpec((rows, 1), lambda j: (0, 0)),
            pl.BlockSpec((direct.shape[0], block), lambda j: (0, j)),
            pl.BlockSpec((other.shape[0], block), lambda j: (0, j + offset)),
        ]
        + [pl.BlockSpec(memory_space=pl.ANY) for _ in held],
        out_specs=out_specs,
        scratch_shapes=[pltpu.VMEM((rows, rows), jnp.bfloat16)],
        input_output_aliases={4: 0} if held else {},
        compiler_params=pltpu.CompilerParams(vmem_limit_bytes=40 * 2**20),
        cost_estimate=pl.CostEstimate(
            flops=4 * rows * rows * width, bytes_accessed=8 * rows * width, transcendentals=0
        ),
        name="place",
    )(where_to.reshape(1, rows), limits.reshape(rows, 1), direct, other, *held)


def pack_both_kernel(to_ref, in_ref, both_ref, rest_ref, matrix):
    block = pl.program_id(0)

    @pl.when(block == 0)
    def _():
        matrix[...] = pick(to_ref[...], matrix.shape[0])

    groups = both_ref.shape[0]
    count, width = rest_ref.shape
    late = in_ref.shape[0] - count
    base = count // groups
    inner = width // EDGE
    value = move(matrix[...], in_ref[...])
    blocks = pl.num_programs(0) * inner // groups
    first = both_ref.shape[1] - late * blocks
    panel_steps = first // base // inner

    @pl.when(block < panel_steps)
    def _():
        for d in range(groups):
            for c in range(inner):
                at = pl.multiple_of((block * inner + c) * base, 8)
                both_ref[d, pl.ds(at, base), :] = value[
                    d * base : (d + 1) * base, c * EDGE : (c + 1) * EDGE
                ]

    @pl.when(block >= panel_steps)
    def _():
        rest_ref[...] = value[:count]

    for c in range(inner):
        at = block * inner + c
        row = pl.multiple_of(first + lax.rem(at, blocks) * late, 8)
        both_ref[lax.div(at, blocks), pl.ds(row, late), :] = value[count:, c * EDGE : (c + 1) * EDGE]


def pack_both(values, where_to, count, groups, panels):
    rows, full = values.shape
    block = block_width(panels)
    steps = panels // block
    size = (count // groups) * (panels // EDGE) + (rows - count) * (full // groups // EDGE)
    return pl.pallas_call(
        pack_both_kernel,
        grid=(full // block,),
        out_shape=[
            jax.ShapeDtypeStruct((groups, size, EDGE), jnp.float32),
            jax.ShapeDtypeStruct((count, full - panels), jnp.float32),
        ],
        in_specs=[
            pl.BlockSpec((1, rows), lambda j: (0, 0)),
            pl.BlockSpec((rows, block), lambda j: (0, j)),
        ],
        out_specs=[
            pl.BlockSpec((groups, size, EDGE), lambda j: (0, 0, 0)),
            pl.BlockSpec((count, block), lambda j: (0, jnp.maximum(j - steps, 0))),
        ],
        scratch_shapes=[pltpu.VMEM((rows, rows), jnp.bfloat16)],
        compiler_params=pltpu.CompilerParams(vmem_limit_bytes=40 * 2**20),
        cost_estimate=pl.CostEstimate(
            flops=4 * rows * rows * full, bytes_accessed=8 * rows * full, transcendentals=0
        ),
        name="pack_both",
    )(where_to.reshape(1, rows), values)


def turn_both_kernel(to_ref, in_ref, out_ref, matrix):
    matrix[...] = pick(to_ref[...], matrix.shape[0])
    groups = in_ref.shape[0]
    late = out_ref.shape[0] // groups
    blocks = out_ref.shape[1] // EDGE
    first = in_ref.shape[1] - late * blocks
    for c in range(blocks):
        at = first + c * late
        value = jnp.concatenate([in_ref[h, at : at + late, :] for h in range(groups)], axis=0)
        out_ref[:, c * EDGE : (c + 1) * EDGE] = move(matrix[...], value)


def turn_both(both, where_to, late, part):
    groups = both.shape[0]
    count = groups * late
    vmem = pl.BlockSpec(memory_space=pltpu.VMEM)
    return pl.pallas_call(
        turn_both_kernel,
        out_shape=jax.ShapeDtypeStruct((count, part), jnp.float32),
        in_specs=[vmem] * 2,
        out_specs=vmem,
        scratch_shapes=[pltpu.VMEM((count, count), jnp.bfloat16)],
        compiler_params=pltpu.CompilerParams(vmem_limit_bytes=40 * 2**20),
        cost_estimate=pl.CostEstimate(
            flops=4 * count * count * part, bytes_accessed=8 * count * part, transcendentals=0
        ),
        name="turn_both",
    )(where_to.reshape(1, count), both)


def place_both_kernel(base, to_ref, limit_ref, both_ref, other_ref, out_ref, panel_ref, matrix):
    block = pl.program_id(0)

    @pl.when(block == 0)
    def _():
        matrix[...] = pick(to_ref[...], matrix.shape[0])

    groups = both_ref.shape[0]
    count = groups * base
    inner = out_ref.shape[1] // EDGE
    for c in range(inner):
        at = pl.multiple_of((block * inner + c) * base, 8)
        own = slice(c * EDGE, (c + 1) * EDGE)
        direct = jnp.concatenate([both_ref[h, pl.ds(at, base), :] for h in range(groups)], axis=0)
        value = move(matrix[:, :count], direct) + move(matrix[:, count:], other_ref[:, own])
        column = lax.broadcasted_iota(jnp.int32, value.shape, 1) + (block * inner + c) * EDGE
        value = jnp.where(column >= limit_ref[...], value, 0.0)
        out_ref[:, own] = value
        panel_ref[:, own] = value


def place_both(both, other, where_to, limits, base, panels):
    rows, full = limits.shape[0], other.shape[1]
    block = block_width(panels)
    return pl.pallas_call(
        functools.partial(place_both_kernel, base),
        grid=(panels // block,),
        out_shape=[
            jax.ShapeDtypeStruct((rows, full), jnp.float32),
            jax.ShapeDtypeStruct((rows, panels), jnp.float32),
        ],
        in_specs=[
            pl.BlockSpec((1, rows), lambda j: (0, 0)),
            pl.BlockSpec((rows, 1), lambda j: (0, 0)),
            pl.BlockSpec(both.shape, lambda j: (0, 0, 0)),
            pl.BlockSpec((other.shape[0], block), lambda j: (0, j)),
        ],
        out_specs=[pl.BlockSpec((rows, block), lambda j: (0, j))] * 2,
        scratch_shapes=[pltpu.VMEM((rows, rows), jnp.bfloat16)],
        compiler_params=pltpu.CompilerParams(vmem_limit_bytes=40 * 2**20),
        cost_estimate=pl.CostEstimate(
            flops=4 * rows * rows * panels, bytes_accessed=8 * rows * panels, transcendentals=0
        ),
        name="place_both",
    )(where_to.reshape(1, rows), limits.reshape(rows, 1), both, other)


def basis_kernel(panel_ref, inverse_ref, high_ref, low_ref):
    value = triple(split(panel_ref[...]), split(inverse_ref[...]), ((1,), (1,)))
    high_ref[...], low_ref[...] = split(value)


def basis_of(panel, inverse):
    rows, panels = panel.shape
    vmem = pl.BlockSpec(memory_space=pltpu.VMEM)
    return pl.pallas_call(
        basis_kernel,
        out_shape=[jax.ShapeDtypeStruct((rows, panels), jnp.bfloat16)] * 2,
        in_specs=[vmem] * 2,
        out_specs=[vmem] * 2,
        compiler_params=pltpu.CompilerParams(vmem_limit_bytes=56 * 2**20),
        cost_estimate=pl.CostEstimate(
            flops=6 * rows * panels * panels,
            bytes_accessed=4 * panels * (2 * rows + panels),
            transcendentals=0,
        ),
        name="basis",
    )(panel, inverse)


def project_kernel(count, where_ref, high_ref, low_ref, front_ref, *rest):
    pieces, rest = rest[:count], rest[count:]
    shares, rest = rest[:count], rest[count:]
    out_ref, factor_ref, one, two = rest[-4:]
    step, part = pl.program_id(0), pl.program_id(1)
    rows = out_ref.shape[0]
    for i in range(count):

        @pl.when((step == i) & (part == 0))
        def _():
            one[...], two[...] = split(pieces[i][...])
            factor_ref[...] = shares[i][...]

    own = pl.ds(pl.multiple_of(part * rows, rows), rows)
    basis = high_ref[own, :], low_ref[own, :]
    out_ref[...] = front_ref[...] - triple(basis, (one[...], two[...]), ((1,), (0,)))


def project(front, factor, basis, pieces, where, me):
    rows, full = front.shape
    panels, width = pieces[0].shape
    count = len(pieces)
    share = panels // lax.axis_size("gr")
    place_at = jnp.stack(list(where) + [me]).astype(jnp.int32)
    held = [] if factor is None else [factor]
    whole = pl.BlockSpec((rows, panels), lambda j, k, at: (0, 0))
    block = pl.BlockSpec((rows // 2, width), lambda j, k, at: (k, at[j]))
    return pl.pallas_call(
        functools.partial(project_kernel, count),
        grid_spec=pltpu.PrefetchScalarGridSpec(
            num_scalar_prefetch=1,
            grid=(count, 2),
            in_specs=[whole, whole, block]
            + [pl.BlockSpec((panels, width), lambda j, k, at: (0, 0)) for _ in pieces]
            + [pl.BlockSpec((share, width), lambda j, k, at: (at[count], 0)) for _ in pieces]
            + [pl.BlockSpec(memory_space=pl.ANY) for _ in held],
            out_specs=[block, pl.BlockSpec((share, width), lambda j, k, at: (0, at[j]))],
            scratch_shapes=[pltpu.VMEM((panels, width), jnp.bfloat16)] * 2,
        ),
        out_shape=[
            jax.ShapeDtypeStruct((rows, full), jnp.float32),
            jax.ShapeDtypeStruct((share, full), jnp.float32),
        ],
        input_output_aliases={3: 0, 4 + 2 * count: 1} if held else {3: 0},
        compiler_params=pltpu.CompilerParams(vmem_limit_bytes=56 * 2**20),
        cost_estimate=pl.CostEstimate(
            flops=6 * rows * panels * width * count,
            bytes_accessed=4 * count * (2 * rows + panels) * width,
            transcendentals=0,
        ),
        name="project",
    )(place_at, *basis, front, *pieces, *pieces, *held)


def pack_plan(row_map, groups, rows_dev, base):
    dest = row_map // rows_dev
    at = jnp.arange(rows_dev, dtype=jnp.int32)
    before = (at[:, None] < at[None, :]).astype(jnp.bfloat16)
    onehot = dest[None, :] == jnp.arange(groups, dtype=jnp.int32)[:, None]
    ahead = dot(onehot.astype(jnp.bfloat16), before, ((1,), (0,)), None)
    rank = jnp.sum(jnp.where(onehot, ahead, 0.0), axis=0).astype(jnp.int32)
    late = rank >= base
    late_rank = dot(late[None, :].astype(jnp.bfloat16), before, ((1,), (0,)), None)[0]
    return jnp.where(late, groups * base + late_rank.astype(jnp.int32), dest * base + rank)


def arrival_plan(every, rows_dev, base):
    me = lax.axis_index("gr")
    groups = every.shape[0]
    other = rows_dev - groups * base
    dest, slot = every // rows_dev, every % rows_dev
    at = jnp.arange(rows_dev, dtype=jnp.int32)
    before = (at[:, None] < at[None, :]).astype(jnp.bfloat16)
    group_ids = jnp.arange(groups, dtype=jnp.int32)
    onehot = dest[:, None, :] == group_ids[None, :, None]
    ahead = dot(
        onehot.reshape(groups * groups, rows_dev).astype(jnp.bfloat16), before, ((1,), (0,)), None
    ).reshape(groups, groups, rows_dev)
    rank = jnp.sum(jnp.where(onehot, ahead, 0.0), axis=1).astype(jnp.int32)
    late = rank >= base
    late_rank = dot(late.astype(jnp.bfloat16), before, ((1,), (0,)), None).astype(jnp.int32)
    sent = jnp.sum(onehot.astype(jnp.int32), axis=2) - base
    earlier = jnp.cumsum(sent, axis=0) - sent
    start = jnp.sum(jnp.where(onehot, earlier[:, :, None], 0), axis=1)
    turn = start + rank - base
    late_ids = jnp.arange(other, dtype=jnp.int32)
    chosen = late[:, None, :] & (late_rank[:, None, :] == late_ids[None, :, None])
    turn_to = jnp.sum(jnp.where(chosen, (dest * other + turn)[:, None, :], 0), axis=2).reshape(-1)
    arrival = jnp.where(late, groups * base + turn, group_ids[:, None] * base + rank)
    arrival = jnp.where(dest == me, arrival, -1).reshape(-1)
    place_to = jnp.sum(
        jnp.where(arrival[None, :] == at[:, None], slot.reshape(-1)[None, :], 0), axis=1
    )
    return turn_to, place_to


def to_all(value):
    return lax.all_to_all(value, "gr", 0, 0, tiled=True)


def turn_rows(spread, turn_to):
    groups, other, part = spread.shape
    return reorder(spread.reshape(groups * other, part), turn_to).reshape(groups, other, part)


def after(value, *others):
    if isinstance(value, (list, tuple)):
        return list(lax.optimization_barrier(tuple(value) + others)[: len(value)])
    return lax.optimization_barrier((value,) + others)[0]


def stages_of(groups, core):
    count = groups.bit_length() - 1
    me = lax.axis_index("gr")
    found = []
    for one, two in zip(range(1, count), range(count - 1, 0, -1)):
        pairs = [(i, i ^ (1 << (two if i & 1 else one))) for i in range(groups)]
        found.append((pairs, jnp.where(core == 1, (me >> two) & 1, (me >> one) & 1)))
    return found


def swap(value):
    groups = lax.axis_size("gr")
    return lax.ppermute(value, "gr", [(i, i ^ 1) for i in range(groups)])


def position(index, stages, core):
    at = core
    for j, (_, mine) in enumerate(stages):
        at = 2 * at + (mine ^ ((index >> (len(stages) - 1 - j)) & 1))
    return at


def chip_pairs(r, planes, chosen):
    groups = lax.axis_size("gr")
    return [
        (i * planes + z, (i ^ (2 * r)) * planes + z) for i in range(groups) for z in chosen
    ]


def reduce_direct(value, planes, chosen):
    chips = lax.axis_size("gr") // 2
    chip = lax.axis_index("gr") // 2
    size = value.shape[0] // chips

    def rows_of(r):
        return lax.dynamic_slice_in_dim(value, (chip ^ r) * size, size, 0)

    came = [
        lax.ppermute(rows_of(r), ("gr", "gc"), chip_pairs(r, planes, chosen))
        for r in range(chips - 1, 0, -1)
    ]
    total = rows_of(0)
    for one in came:
        total = total + one
    return total


def gather_direct(value, planes, wait):
    chips = lax.axis_size("gr") // 2
    every = range(planes)
    came = [
        lax.ppermute(value, ("gr", "gc"), chip_pairs(r, planes, every)) for r in range(1, chips)
    ]
    came = after(came, *wait)
    return jnp.concatenate([value] + came, axis=0)


def send_stage(pieces, j):
    groups = lax.axis_size("gr")
    stages = stages_of(groups, lax.axis_index("gr") & 1)
    bit = 1 << (len(stages) - 1 - j)
    order = sorted((i for i in pieces if i & bit), reverse=True)
    came = [lax.ppermute(pieces[i], "gr", stages[j][0]) for i in order]
    return {i ^ bit: pieces[i ^ bit] for i in order}, came


def add_stage(left, came):
    return {i: left[i] + one for i, one in zip(left, came)}


def pieces_of(value):
    stages = stages_of(lax.axis_size("gr"), lax.axis_index("gr") & 1)
    size = value.shape[0] >> len(stages)
    return {
        i: lax.dynamic_slice_in_dim(value, position(i, stages, jnp.int32(0)) * size, size, 0)
        for i in range(1 << len(stages))
    }


def gather_pieces(piece, use):
    core = lax.axis_index("gr") & 1
    stages, others = stages_of(lax.axis_size("gr"), core), stages_of(lax.axis_size("gr"), 1 - core)
    pieces = {0: piece}

    def take(i):
        return use(
            [pieces[i], swap(pieces[i])],
            [position(i, stages, core), position(i, others, 1 - core)],
        )

    for j in range(len(stages) - 1, -1, -1):
        bit = 1 << (len(stages) - 1 - j)
        pieces[bit] = lax.ppermute(piece, "gr", stages[j][0])
    done = take(0)
    for i in pieces:
        pieces[i] = after(pieces[i], done)
    for j in range(len(stages) - 2, -1, -1):
        bit = 1 << (len(stages) - 1 - j)
        for i in range(1, bit):
            pieces[i | bit] = lax.ppermute(pieces[i], "gr", stages[j][0])
    for i in sorted(i for i in pieces if i):
        pieces[i] = after(pieces[i], done) if i == len(pieces) - 1 else pieces[i]
        done = take(i)


def hop(value, step, planes, *wait):
    me = lax.axis_index("gc")
    pairs = [(i, i + step) for i in range(0, planes, 2 * step)]
    came = after(lax.ppermute(value, "gc", pairs), *wait)
    return jnp.where(me % (2 * step) == step, came, value)


def steps_of(planes):
    return [planes >> i for i in range(1, planes.bit_length())]


def shards(child_rows, row_map, stair):
    groups, planes = lax.axis_size("gr"), lax.axis_size("gc")
    me, plane = lax.axis_index("gr"), lax.axis_index("gc")
    core = me & 1
    rows_dev, cols_dev = child_rows.shape
    panels = NPANEL * PANEL
    half = cols_dev // 2
    blocks = panels // EDGE
    base = 3 * rows_dev // (4 * groups)
    columns = jnp.arange(cols_dev, dtype=jnp.int32)
    stair_ids = jnp.arange(stair.shape[0], dtype=jnp.int32)
    child_limits = jnp.sum(
        jnp.where((row_map // STAIR_BLOCK)[:, None] == stair_ids[None, :], stair[None, :], 0), axis=1
    )
    child_limits = child_limits - plane * cols_dev
    own_blocks = rows_dev // STAIR_BLOCK
    limits = jnp.repeat(
        lax.dynamic_slice_in_dim(stair, me * own_blocks, own_blocks, 0), STAIR_BLOCK
    )
    limits = limits - plane * cols_dev
    everyone = range(planes)

    panel = jnp.where(columns[None, :panels] >= child_limits[:, None], child_rows[:, :panels], 0.0)
    pair = jnp.concatenate([panel, swap(panel)], axis=0)


    quarter = panels // 4
    outer = jnp.concatenate([pair[:, :quarter], pair[:, 3 * quarter :]], axis=1)
    share = jnp.where(core == 0, outer, pair[:, quarter : 3 * quarter])
    gram = dot(share, pair, ((0,), (0,)), HIGHEST)
    packed = []
    for lead in (0, blocks // 4):
        rows = []
        for i in range(blocks // 4):
            one, two = lead + i + 1, blocks - lead - i
            last = blocks // 2 - 1 - i
            rows.append(
                jnp.concatenate(
                    [
                        gram[i * EDGE : (i + 1) * EDGE, : one * EDGE],
                        gram[last * EDGE : (last + 1) * EDGE, : two * EDGE],
                    ],
                    axis=1,
                )
            )
        packed.append(jnp.concatenate(rows, axis=0))
    gram = jnp.where(core == 0, packed[0], packed[1])
    gram_sum = reduce_direct(gram, planes, [0])
    count = groups * base
    every = to_all(after(jnp.broadcast_to(row_map[None, :], (groups, rows_dev)), gram))
    pack_to = pack_plan(row_map, groups, rows_dev, base)
    part, late = cols_dev // groups, rows_dev - count
    joint = part % EDGE == 0 and cols_dev % panels == 0 and cols_dev > panels
    if joint:
        sent, rest = pack_both(child_rows, after(pack_to, gram), count, groups, panels)
        both = to_all(after(sent, gram_sum))
    else:
        direct, spread = pack(child_rows, after(pack_to, gram), count)
        spread = to_all(spread.reshape(late, groups, -1).transpose(1, 0, 2))
        direct = to_all(direct.reshape(groups, base, cols_dev)).reshape(count, cols_dev)
    steps = steps_of(planes)
    gram_first, everywhere = gram_sum, panel
    for step in steps:
        gram_first = hop(gram_first, step, planes)
        if step > 1:
            everywhere = hop(everywhere, step, planes, gram_first)

    turn_to, place_to = arrival_plan(every, rows_dev, base)
    turn_to, place_to = lax.optimization_barrier((turn_to, place_to))
    if joint:
        both = after(both, everywhere)
        spread = turn_both(both, turn_to, late, part).reshape(groups, late, part)
    else:
        spread = turn_rows(spread, turn_to)

    halves = []
    child = after(child_rows, gram_first)
    for start in (core * half, (1 - core) * half):
        value = lax.dynamic_slice_in_dim(child, start, half, 1)
        halves.append(jnp.where(start + columns[None, :half] >= child_limits[:, None], value, 0.0))
    other = swap(halves[1])
    gram = gather_direct(gram_first, planes, (spread, halves[0], halves[1]))
    grams = [jnp.stack([core, me // 2]).astype(jnp.int32), gram, swap(gram)]
    spread = to_all(spread)

    everywhere = hop(everywhere, 1, planes, gram, spread)
    spread = spread.transpose(1, 0, 2).reshape(late, cols_dev)
    if joint:
        front, own_panel = place_both(both, spread, place_to, limits, base, panels)
    else:
        front, own_panel = place(direct, spread, place_to, limits, None, 0)
        own_panel = own_panel[:, :panels]

    product = dot(halves[0], after(everywhere, own_panel), ((0,), (0,)), HIGH)
    product += dot(other, swap(everywhere), ((0,), (0,)), HIGH)
    product, came = send_stage(pieces_of(product), 0)
    grams = after(grams, own_panel, *product.values())
    inverse = inverse_factor(grams, panels, 0, blocks // 2, groups // 2)
    came[0] = after(came[0], inverse)
    own_panel = hop(own_panel, steps[0], planes, came[0])
    for i in range(1, len(came)):
        came[i] = after(came[i], inverse)
    stages = groups.bit_length() - 2
    product = add_stage(product, came)
    sent = send_stage(product, 1) if stages > 1 else None
    second = None
    if joint:
        second = after(rest, product[max(product)])
        second = to_all(second.reshape(groups, base, -1)).reshape(count, -1)
    inverse = inverse_factor(
        [after(inverse, own_panel, product[max(product)])], panels, blocks // 2, blocks, groups // 2
    )
    for j in range(1, stages):
        left, came = sent if j == 1 else send_stage(product, j)
        product = add_stage(left, [after(one, inverse) for one in came])
    product = product[0]
    for step in steps[1:]:
        own_panel = hop(own_panel, step, planes, inverse)
    coupling = dot(inverse, product, ((1,), (1,)), HIGH)
    basis = basis_of(own_panel, inverse)
    if joint:
        (front,) = place(second, spread, after(place_to, coupling), limits, front, panels)
    piece_cols = coupling.shape[1]
    if piece_cols % EDGE == 0:
        held = [front, None]

        def use(pieces, where):
            held[:] = project(held[0], held[1], basis, pieces, where, me)
            return held[1]

        gather_pieces(coupling, use)
        return (held[1], held[0])
    held = [jnp.zeros((panels, cols_dev), jnp.float32)]

    def keep(pieces, where):
        for piece, at in zip(pieces, where):
            held[0] = lax.dynamic_update_slice_in_dim(held[0], piece, at * piece_cols, 1)
        return pieces[0]

    gather_pieces(coupling, keep)
    whole = held[0]
    share_rows = panels // groups
    factor = lax.dynamic_slice_in_dim(whole, me * share_rows, share_rows, 0)
    basis = basis[0].astype(jnp.float32) + basis[1].astype(jnp.float32)
    return (factor, front - dot(basis, whole, ((1,), (0,)), HIGH))


def solution(mesh):
    placed = (P("gr", "gc"), P("gr"), P())
    return jax.shard_map(
        shards,
        mesh=mesh,
        in_specs=placed,
        out_specs=(P("gr", "gc"), P("gr", "gc")),
        check_vma=False,
    )
```

```python
import functools

import jax
import jax.numpy as jnp
from jax import lax
from jax.experimental import pallas as pl
from jax.experimental.pallas import tpu as pltpu
from jax.sharding import PartitionSpec as P

PANEL = 512
NPANEL = 2
STAIR_BLOCK = 128
EDGE = 128
HIGHEST = lax.Precision.HIGHEST
HIGH = lax.Precision.HIGH


def dot(left, right, dims, precision):
    return lax.dot_general(
        left, right, (dims, ((), ())), precision=precision, preferred_element_type=jnp.float32
    )


def split(value):
    high = value.astype(jnp.bfloat16)
    return high, (value - high.astype(jnp.float32)).astype(jnp.bfloat16)


def triple(left, right, dims):
    small = dot(left[0], right[1], dims, None) + dot(left[1], right[0], dims, None)
    return small + dot(left[0], right[0], dims, None)


def eliminate(tiles):
    lane = lax.broadcasted_iota(jnp.int32, (8, EDGE), 1)
    sub = lax.broadcasted_iota(jnp.int32, (8, EDGE), 0)
    tiles = list(tiles)
    strips = len(tiles)
    for strip in range(strips):
        first = 8 * strip
        own = (lane >= first) & (lane < first + 8)
        mult = {
            t: [jnp.broadcast_to(tiles[t][:, first + s : first + s + 1], (8, EDGE)) for s in range(8)]
            for t in range(strip, strips)
        }
        small = [
            [jnp.broadcast_to(mult[strip][s][t : t + 1, :], (8, EDGE)) for s in range(t + 1)]
            for t in range(8)
        ]
        start = jnp.where(own, jnp.where(lane - first == sub, 1.0, 0.0), tiles[strip])
        rows = [jnp.broadcast_to(start[s : s + 1, :], (8, EDGE)) for s in range(8)]
        inv = [None] * 8
        low = [[None] * 8 for _ in range(8)]
        for s in range(8):
            inv[s] = 1.0 / small[s][s]
            for t in range(s + 1, 8):
                low[t][s] = small[t][s] * inv[s]
                for u in range(s + 1, t + 1):
                    small[t][u] = small[t][u] - low[t][s] * small[u][s]
            for t in range(s + 1, 8):
                rows[t] = rows[t] - low[t][s] * rows[s]
        back = [None] * 8
        for s in range(7, -1, -1):
            value = rows[s] * inv[s]
            for t in range(7, s, -1):
                value = value - low[t][s] * back[t]
            back[s] = value
        out, pivot = rows[7], small[7][7]
        for s in range(6, -1, -1):
            out = jnp.where(sub == s, rows[s], out)
            pivot = jnp.where(sub == s, small[s][s], pivot)
        tiles[strip] = out * lax.rsqrt(pivot)
        for t in range(strip + 1, strips):
            value = jnp.where(own, 0.0, tiles[t])
            for s in range(8):
                value = value - mult[t][s] * back[s]
            tiles[t] = value
    return tiles


def unpack(where_ref, chips, halves, work):
    size = work.shape[0]
    blocks = size // EDGE
    for which, half in enumerate(halves):
        core = where_ref[0] ^ which
        rows = half.shape[0] // chips
        for r in range(chips):
            first = (where_ref[1] ^ r) * rows
            pair = core * (blocks // 4) + first // EDGE
            inside = first % EDGE
            for b in range(blocks + 1):
                lead = b <= pair
                row = jnp.where(lead, pair, blocks - 1 - pair)
                col = jnp.where(lead, b, b - pair - 1)
                work[
                    pl.ds(pl.multiple_of(row * EDGE + inside, 8), rows),
                    pl.ds(pl.multiple_of(col * EDGE, EDGE), EDGE),
                ] = half[r * rows : (r + 1) * rows, b * EDGE : (b + 1) * EDGE]
    for i in range(blocks):
        for j in range(i):
            work[j * EDGE : (j + 1) * EDGE, i * EDGE : (i + 1) * EDGE] = work[
                i * EDGE : (i + 1) * EDGE, j * EDGE : (j + 1) * EDGE
            ].T


def inverse_factor_kernel(first, last, chips, *refs):
    out_ref, work, high, low = refs[-4:]
    size = work.shape[0]
    blocks = size // EDGE
    if first == 0:
        unpack(refs[0], chips, refs[1:-4], work)
    else:
        work[...] = refs[0][...]
    lower = lax.broadcasted_iota(jnp.int32, (EDGE, EDGE), 0) >= lax.broadcasted_iota(
        jnp.int32, (EDGE, EDGE), 1
    )

    @pl.loop(first, last)
    def _(k):
        at = pl.multiple_of(k * EDGE, EDGE)
        tiles = [
            work[pl.ds(pl.multiple_of(at + 8 * t, 8), 8), pl.ds(at, EDGE)] for t in range(EDGE // 8)
        ]
        diag = jnp.where(lower, jnp.concatenate(eliminate(tiles), axis=0), 0.0)
        work[pl.ds(at, EDGE), :] = triple(split(diag), split(work[pl.ds(at, EDGE), :]), ((1,), (0,)))
        work[pl.ds(at, EDGE), pl.ds(at, EDGE)] = diag
        high[...], low[...] = split(work[pl.ds(at, EDGE), :])

        @pl.loop(k + 1, blocks)
        def _(i):
            below = pl.multiple_of(i * EDGE, EDGE)
            coeff = high[:, pl.ds(below, EDGE)], low[:, pl.ds(below, EDGE)]
            work[pl.ds(below, EDGE), pl.ds(at, EDGE)] = jnp.zeros((EDGE, EDGE), jnp.float32)
            work[pl.ds(below, EDGE), :] -= triple(coeff, (high[...], low[...]), ((0,), (0,)))

    if last == blocks:
        for k in range(blocks - 1):
            work[k * EDGE : (k + 1) * EDGE, (k + 1) * EDGE :] = jnp.zeros(
                (EDGE, size - (k + 1) * EDGE), jnp.float32
            )
    out_ref[...] = work[...]


def inverse_factor(held, size, first, last, chips):
    vmem = pl.BlockSpec(memory_space=pltpu.VMEM)
    specs = [vmem] if first else [pl.BlockSpec(memory_space=pltpu.SMEM), vmem, vmem]
    return pl.pallas_call(
        functools.partial(inverse_factor_kernel, first, last, chips),
        out_shape=jax.ShapeDtypeStruct((size, size), jnp.float32),
        in_specs=specs,
        out_specs=vmem,
        scratch_shapes=[pltpu.VMEM((size, size), jnp.float32)]
        + [pltpu.VMEM((EDGE, size), jnp.bfloat16)] * 2,
        compiler_params=pltpu.CompilerParams(vmem_limit_bytes=40 * 2**20),
        cost_estimate=pl.CostEstimate(
            flops=32 * size**3, bytes_accessed=32 * size * size, transcendentals=size
        ),
        name="inverse_factor",
    )(*held)


def pick(where_to, count):
    rows = lax.broadcasted_iota(jnp.int32, (count, where_to.shape[1]), 0)
    return jnp.where(rows == where_to, 1.0, 0.0).astype(jnp.bfloat16)


def move(matrix, values):
    high = values.astype(jnp.bfloat16)
    rest = (values - high.astype(jnp.float32)).astype(jnp.bfloat16)
    dims = ((1,), (0,))
    return dot(matrix, high, dims, None) + dot(matrix, rest, dims, None)


def reorder_kernel(to_ref, in_ref, out_ref, matrix):
    matrix[...] = pick(to_ref[...], matrix.shape[0])
    out_ref[...] = move(matrix[...], in_ref[...])


def reorder(values, where_to):
    count, width = values.shape
    return pl.pallas_call(
        reorder_kernel,
        out_shape=jax.ShapeDtypeStruct((count, width), jnp.float32),
        in_specs=[pl.BlockSpec(memory_space=pltpu.VMEM)] * 2,
        out_specs=pl.BlockSpec(memory_space=pltpu.VMEM),
        scratch_shapes=[pltpu.VMEM((count, count), jnp.bfloat16)],
        compiler_params=pltpu.CompilerParams(vmem_limit_bytes=40 * 2**20),
        cost_estimate=pl.CostEstimate(
            flops=4 * count * count * width, bytes_accessed=8 * count * width, transcendentals=0
        ),
        name="reorder",
    )(where_to.reshape(1, count), values)


def block_width(width):
    for block in (512, 384, 256, 128):
        if width % block == 0:
            return block
    return width


def pack_kernel(to_ref, in_ref, direct_ref, other_ref, matrix):
    @pl.when(pl.program_id(0) == 0)
    def _():
        matrix[...] = pick(to_ref[...], matrix.shape[0])

    count = direct_ref.shape[0]
    value = move(matrix[...], in_ref[...])
    direct_ref[...] = value[:count]
    other_ref[...] = value[count:]


def pack(values, where_to, count):
    rows, width = values.shape
    block = block_width(width)
    return pl.pallas_call(
        pack_kernel,
        grid=(width // block,),
        out_shape=[
            jax.ShapeDtypeStruct((count, width), jnp.float32),
            jax.ShapeDtypeStruct((rows - count, width), jnp.float32),
        ],
        in_specs=[
            pl.BlockSpec((1, rows), lambda j: (0, 0)),
            pl.BlockSpec((rows, block), lambda j: (0, j)),
        ],
        out_specs=[
            pl.BlockSpec((count, block), lambda j: (0, j)),
            pl.BlockSpec((rows - count, block), lambda j: (0, j)),
        ],
        scratch_shapes=[pltpu.VMEM((rows, rows), jnp.bfloat16)],
        compiler_params=pltpu.CompilerParams(vmem_limit_bytes=40 * 2**20),
        cost_estimate=pl.CostEstimate(
            flops=4 * rows * rows * width, bytes_accessed=8 * rows * width, transcendentals=0
        ),
        name="pack",
    )(where_to.reshape(1, rows), values)


def place_kernel(offset, outs, to_ref, limit_ref, direct_ref, other_ref, *rest):
    out_refs, matrix = rest[len(rest) - 1 - outs : -1], rest[-1]
    block = pl.program_id(0)

    @pl.when(block == 0)
    def _():
        matrix[...] = pick(to_ref[...], matrix.shape[0])

    count = direct_ref.shape[0]
    value = move(matrix[:, :count], direct_ref[...]) + move(matrix[:, count:], other_ref[...])
    column = lax.broadcasted_iota(jnp.int32, value.shape, 1) + (block + offset) * value.shape[1]
    for out_ref in out_refs:
        out_ref[...] = jnp.where(column >= limit_ref[...], value, 0.0)


def place(direct, other, where_to, limits, front, start):
    rows = limits.shape[0]
    width, full = direct.shape[1], other.shape[1]
    block = block_width(width)
    offset = start // block
    held = [] if front is None else [front]
    outs = [jax.ShapeDtypeStruct((rows, full), jnp.float32)]
    out_specs = [pl.BlockSpec((rows, block), lambda j: (0, j + offset))]
    if not held:
        outs.append(jax.ShapeDtypeStruct((rows, width), jnp.float32))
        out_specs.append(pl.BlockSpec((rows, block), lambda j: (0, j)))
    return pl.pallas_call(
        functools.partial(place_kernel, offset, len(outs)),
        grid=(width // block,),
        out_shape=outs,
        in_specs=[
            pl.BlockSpec((1, rows), lambda j: (0, 0)),
            pl.BlockSpec((rows, 1), lambda j: (0, 0)),
            pl.BlockSpec((direct.shape[0], block), lambda j: (0, j)),
            pl.BlockSpec((other.shape[0], block), lambda j: (0, j + offset)),
        ]
        + [pl.BlockSpec(memory_space=pl.ANY) for _ in held],
        out_specs=out_specs,
        scratch_shapes=[pltpu.VMEM((rows, rows), jnp.bfloat16)],
        input_output_aliases={4: 0} if held else {},
        compiler_params=pltpu.CompilerParams(vmem_limit_bytes=40 * 2**20),
        cost_estimate=pl.CostEstimate(
            flops=4 * rows * rows * width, bytes_accessed=8 * rows * width, transcendentals=0
        ),
        name="place",
    )(where_to.reshape(1, rows), limits.reshape(rows, 1), direct, other, *held)


def pack_both_kernel(to_ref, in_ref, both_ref, rest_ref, matrix):
    block = pl.program_id(0)

    @pl.when(block == 0)
    def _():
        matrix[...] = pick(to_ref[...], matrix.shape[0])

    groups = both_ref.shape[0]
    count, width = rest_ref.shape
    late = in_ref.shape[0] - count
    base = count // groups
    inner = width // EDGE
    value = move(matrix[...], in_ref[...])
    blocks = pl.num_programs(0) * inner // groups
    first = both_ref.shape[1] - late * blocks
    panel_steps = first // base // inner

    @pl.when(block < panel_steps)
    def _():
        for d in range(groups):
            for c in range(inner):
                at = pl.multiple_of((block * inner + c) * base, 8)
                both_ref[d, pl.ds(at, base), :] = value[
                    d * base : (d + 1) * base, c * EDGE : (c + 1) * EDGE
                ]

    @pl.when(block >= panel_steps)
    def _():
        rest_ref[...] = value[:count]

    for c in range(inner):
        at = block * inner + c
        row = pl.multiple_of(first + lax.rem(at, blocks) * late, 8)
        both_ref[lax.div(at, blocks), pl.ds(row, late), :] = value[count:, c * EDGE : (c + 1) * EDGE]


def pack_both(values, where_to, count, groups, panels):
    rows, full = values.shape
    block = block_width(panels)
    steps = panels // block
    size = (count // groups) * (panels // EDGE) + (rows - count) * (full // groups // EDGE)
    return pl.pallas_call(
        pack_both_kernel,
        grid=(full // block,),
        out_shape=[
            jax.ShapeDtypeStruct((groups, size, EDGE), jnp.float32),
            jax.ShapeDtypeStruct((count, full - panels), jnp.float32),
        ],
        in_specs=[
            pl.BlockSpec((1, rows), lambda j: (0, 0)),
            pl.BlockSpec((rows, block), lambda j: (0, j)),
        ],
        out_specs=[
            pl.BlockSpec((groups, size, EDGE), lambda j: (0, 0, 0)),
            pl.BlockSpec((count, block), lambda j: (0, jnp.maximum(j - steps, 0))),
        ],
        scratch_shapes=[pltpu.VMEM((rows, rows), jnp.bfloat16)],
        compiler_params=pltpu.CompilerParams(vmem_limit_bytes=40 * 2**20),
        cost_estimate=pl.CostEstimate(
            flops=4 * rows * rows * full, bytes_accessed=8 * rows * full, transcendentals=0
        ),
        name="pack_both",
    )(where_to.reshape(1, rows), values)


def turn_both_kernel(to_ref, in_ref, out_ref, matrix):
    matrix[...] = pick(to_ref[...], matrix.shape[0])
    groups = in_ref.shape[0]
    late = out_ref.shape[0] // groups
    blocks = out_ref.shape[1] // EDGE
    first = in_ref.shape[1] - late * blocks
    for c in range(blocks):
        at = first + c * late
        value = jnp.concatenate([in_ref[h, at : at + late, :] for h in range(groups)], axis=0)
        out_ref[:, c * EDGE : (c + 1) * EDGE] = move(matrix[...], value)


def turn_both(both, where_to, late, part):
    groups = both.shape[0]
    count = groups * late
    vmem = pl.BlockSpec(memory_space=pltpu.VMEM)
    return pl.pallas_call(
        turn_both_kernel,
        out_shape=jax.ShapeDtypeStruct((count, part), jnp.float32),
        in_specs=[vmem] * 2,
        out_specs=vmem,
        scratch_shapes=[pltpu.VMEM((count, count), jnp.bfloat16)],
        compiler_params=pltpu.CompilerParams(vmem_limit_bytes=40 * 2**20),
        cost_estimate=pl.CostEstimate(
            flops=4 * count * count * part, bytes_accessed=8 * count * part, transcendentals=0
        ),
        name="turn_both",
    )(where_to.reshape(1, count), both)


def place_both_kernel(base, to_ref, limit_ref, both_ref, other_ref, out_ref, panel_ref, matrix):
    block = pl.program_id(0)

    @pl.when(block == 0)
    def _():
        matrix[...] = pick(to_ref[...], matrix.shape[0])

    groups = both_ref.shape[0]
    count = groups * base
    inner = out_ref.shape[1] // EDGE
    for c in range(inner):
        at = pl.multiple_of((block * inner + c) * base, 8)
        own = slice(c * EDGE, (c + 1) * EDGE)
        direct = jnp.concatenate([both_ref[h, pl.ds(at, base), :] for h in range(groups)], axis=0)
        value = move(matrix[:, :count], direct) + move(matrix[:, count:], other_ref[:, own])
        column = lax.broadcasted_iota(jnp.int32, value.shape, 1) + (block * inner + c) * EDGE
        value = jnp.where(column >= limit_ref[...], value, 0.0)
        out_ref[:, own] = value
        panel_ref[:, own] = value


def place_both(both, other, where_to, limits, base, panels):
    rows, full = limits.shape[0], other.shape[1]
    block = block_width(panels)
    return pl.pallas_call(
        functools.partial(place_both_kernel, base),
        grid=(panels // block,),
        out_shape=[
            jax.ShapeDtypeStruct((rows, full), jnp.float32),
            jax.ShapeDtypeStruct((rows, panels), jnp.float32),
        ],
        in_specs=[
            pl.BlockSpec((1, rows), lambda j: (0, 0)),
            pl.BlockSpec((rows, 1), lambda j: (0, 0)),
            pl.BlockSpec(both.shape, lambda j: (0, 0, 0)),
            pl.BlockSpec((other.shape[0], block), lambda j: (0, j)),
        ],
        out_specs=[pl.BlockSpec((rows, block), lambda j: (0, j))] * 2,
        scratch_shapes=[pltpu.VMEM((rows, rows), jnp.bfloat16)],
        compiler_params=pltpu.CompilerParams(vmem_limit_bytes=40 * 2**20),
        cost_estimate=pl.CostEstimate(
            flops=4 * rows * rows * panels, bytes_accessed=8 * rows * panels, transcendentals=0
        ),
        name="place_both",
    )(where_to.reshape(1, rows), limits.reshape(rows, 1), both, other)


def basis_kernel(panel_ref, inverse_ref, high_ref, low_ref):
    value = triple(split(panel_ref[...]), split(inverse_ref[...]), ((1,), (1,)))
    high_ref[...], low_ref[...] = split(value)


def basis_of(panel, inverse):
    rows, panels = panel.shape
    vmem = pl.BlockSpec(memory_space=pltpu.VMEM)
    return pl.pallas_call(
        basis_kernel,
        out_shape=[jax.ShapeDtypeStruct((rows, panels), jnp.bfloat16)] * 2,
        in_specs=[vmem] * 2,
        out_specs=[vmem] * 2,
        compiler_params=pltpu.CompilerParams(vmem_limit_bytes=56 * 2**20),
        cost_estimate=pl.CostEstimate(
            flops=6 * rows * panels * panels,
            bytes_accessed=4 * panels * (2 * rows + panels),
            transcendentals=0,
        ),
        name="basis",
    )(panel, inverse)


def project_kernel(count, where_ref, high_ref, low_ref, front_ref, *rest):
    pieces, (out_ref, factor_ref) = rest[:count], rest[-2:]
    step = pl.program_id(0)
    share = factor_ref.shape[0]
    own = pl.ds(pl.multiple_of(where_ref[count] * share, share), share)
    for i in range(count):

        @pl.when(step == i)
        def _():
            factor_ref[...] = pieces[i][own, :]
            update = triple((high_ref[...], low_ref[...]), split(pieces[i][...]), ((1,), (0,)))
            out_ref[...] = front_ref[...] - update


def project(front, factor, basis, pieces, where, me):
    rows, full = front.shape
    panels, width = pieces[0].shape
    count = len(pieces)
    share = panels // lax.axis_size("gr")
    place_at = jnp.stack(list(where) + [me]).astype(jnp.int32)
    held = [] if factor is None else [factor]
    whole = pl.BlockSpec((rows, panels), lambda j, at: (0, 0))
    block = pl.BlockSpec((rows, width), lambda j, at: (0, at[j]))
    return pl.pallas_call(
        functools.partial(project_kernel, count),
        grid_spec=pltpu.PrefetchScalarGridSpec(
            num_scalar_prefetch=1,
            grid=(count,),
            in_specs=[whole, whole, block]
            + [pl.BlockSpec((panels, width), lambda j, at: (0, 0)) for _ in pieces]
            + [pl.BlockSpec(memory_space=pl.ANY) for _ in held],
            out_specs=[block, pl.BlockSpec((share, width), lambda j, at: (0, at[j]))],
        ),
        out_shape=[
            jax.ShapeDtypeStruct((rows, full), jnp.float32),
            jax.ShapeDtypeStruct((share, full), jnp.float32),
        ],
        input_output_aliases={3: 0, 4 + count: 1} if held else {3: 0},
        compiler_params=pltpu.CompilerParams(vmem_limit_bytes=56 * 2**20),
        cost_estimate=pl.CostEstimate(
            flops=6 * rows * panels * width * count,
            bytes_accessed=4 * count * (2 * rows + panels) * width,
            transcendentals=0,
        ),
        name="project",
    )(place_at, *basis, front, *pieces, *held)


def pack_plan(row_map, groups, rows_dev, base):
    dest = row_map // rows_dev
    at = jnp.arange(rows_dev, dtype=jnp.int32)
    before = (at[:, None] < at[None, :]).astype(jnp.bfloat16)
    onehot = dest[None, :] == jnp.arange(groups, dtype=jnp.int32)[:, None]
    ahead = dot(onehot.astype(jnp.bfloat16), before, ((1,), (0,)), None)
    rank = jnp.sum(jnp.where(onehot, ahead, 0.0), axis=0).astype(jnp.int32)
    late = rank >= base
    late_rank = dot(late[None, :].astype(jnp.bfloat16), before, ((1,), (0,)), None)[0]
    return jnp.where(late, groups * base + late_rank.astype(jnp.int32), dest * base + rank)


def arrival_plan(every, rows_dev, base):
    me = lax.axis_index("gr")
    groups = every.shape[0]
    other = rows_dev - groups * base
    dest, slot = every // rows_dev, every % rows_dev
    at = jnp.arange(rows_dev, dtype=jnp.int32)
    before = (at[:, None] < at[None, :]).astype(jnp.bfloat16)
    group_ids = jnp.arange(groups, dtype=jnp.int32)
    onehot = dest[:, None, :] == group_ids[None, :, None]
    ahead = dot(
        onehot.reshape(groups * groups, rows_dev).astype(jnp.bfloat16), before, ((1,), (0,)), None
    ).reshape(groups, groups, rows_dev)
    rank = jnp.sum(jnp.where(onehot, ahead, 0.0), axis=1).astype(jnp.int32)
    late = rank >= base
    late_rank = dot(late.astype(jnp.bfloat16), before, ((1,), (0,)), None).astype(jnp.int32)
    sent = jnp.sum(onehot.astype(jnp.int32), axis=2) - base
    earlier = jnp.cumsum(sent, axis=0) - sent
    start = jnp.sum(jnp.where(onehot, earlier[:, :, None], 0), axis=1)
    turn = start + rank - base
    late_ids = jnp.arange(other, dtype=jnp.int32)
    chosen = late[:, None, :] & (late_rank[:, None, :] == late_ids[None, :, None])
    turn_to = jnp.sum(jnp.where(chosen, (dest * other + turn)[:, None, :], 0), axis=2).reshape(-1)
    arrival = jnp.where(late, groups * base + turn, group_ids[:, None] * base + rank)
    arrival = jnp.where(dest == me, arrival, -1).reshape(-1)
    place_to = jnp.sum(
        jnp.where(arrival[None, :] == at[:, None], slot.reshape(-1)[None, :], 0), axis=1
    )
    return turn_to, place_to


def to_all(value):
    return lax.all_to_all(value, "gr", 0, 0, tiled=True)


def turn_rows(spread, turn_to):
    groups, other, part = spread.shape
    return reorder(spread.reshape(groups * other, part), turn_to).reshape(groups, other, part)


def after(value, *others):
    if isinstance(value, (list, tuple)):
        return list(lax.optimization_barrier(tuple(value) + others)[: len(value)])
    return lax.optimization_barrier((value,) + others)[0]


def stages_of(groups, core):
    count = groups.bit_length() - 1
    me = lax.axis_index("gr")
    found = []
    for one, two in zip(range(1, count), range(count - 1, 0, -1)):
        pairs = [(i, i ^ (1 << (two if i & 1 else one))) for i in range(groups)]
        found.append((pairs, jnp.where(core == 1, (me >> two) & 1, (me >> one) & 1)))
    return found


def swap(value):
    groups = lax.axis_size("gr")
    return lax.ppermute(value, "gr", [(i, i ^ 1) for i in range(groups)])


def position(index, stages, core):
    at = core
    for j, (_, mine) in enumerate(stages):
        at = 2 * at + (mine ^ ((index >> (len(stages) - 1 - j)) & 1))
    return at


def chip_pairs(r, planes, chosen):
    groups = lax.axis_size("gr")
    return [
        (i * planes + z, (i ^ (2 * r)) * planes + z) for i in range(groups) for z in chosen
    ]


def reduce_direct(value, planes, chosen):
    chips = lax.axis_size("gr") // 2
    chip = lax.axis_index("gr") // 2
    size = value.shape[0] // chips

    def rows_of(r):
        return lax.dynamic_slice_in_dim(value, (chip ^ r) * size, size, 0)

    came = [
        lax.ppermute(rows_of(r), ("gr", "gc"), chip_pairs(r, planes, chosen))
        for r in range(chips - 1, 0, -1)
    ]
    total = rows_of(0)
    for one in came:
        total = total + one
    return total


def gather_direct(value, planes, wait):
    chips = lax.axis_size("gr") // 2
    every = range(planes)
    came = [
        lax.ppermute(value, ("gr", "gc"), chip_pairs(r, planes, every)) for r in range(1, chips)
    ]
    came = after(came, *wait)
    return jnp.concatenate([value] + came, axis=0)


def send_stage(pieces, j):
    groups = lax.axis_size("gr")
    stages = stages_of(groups, lax.axis_index("gr") & 1)
    bit = 1 << (len(stages) - 1 - j)
    order = sorted((i for i in pieces if i & bit), reverse=True)
    came = [lax.ppermute(pieces[i], "gr", stages[j][0]) for i in reversed(order)][::-1]
    return {i ^ bit: pieces[i ^ bit] for i in order}, came


def add_stage(left, came):
    return {i: left[i] + one for i, one in zip(left, came)}


def pieces_of(value):
    stages = stages_of(lax.axis_size("gr"), lax.axis_index("gr") & 1)
    size = value.shape[0] >> len(stages)
    return {
        i: lax.dynamic_slice_in_dim(value, position(i, stages, jnp.int32(0)) * size, size, 0)
        for i in range(1 << len(stages))
    }


def gather_pieces(piece, use):
    core = lax.axis_index("gr") & 1
    stages, others = stages_of(lax.axis_size("gr"), core), stages_of(lax.axis_size("gr"), 1 - core)
    pieces = {0: piece}

    def take(i):
        return use(
            [pieces[i], swap(pieces[i])],
            [position(i, stages, core), position(i, others, 1 - core)],
        )

    for j in range(len(stages) - 1, -1, -1):
        bit = 1 << (len(stages) - 1 - j)
        pieces[bit] = lax.ppermute(piece, "gr", stages[j][0])
    done = take(0)
    for i in pieces:
        pieces[i] = after(pieces[i], done)
    for j in range(len(stages) - 2, -1, -1):
        bit = 1 << (len(stages) - 1 - j)
        for i in range(1, bit):
            pieces[i | bit] = lax.ppermute(pieces[i], "gr", stages[j][0])
    for i in sorted(i for i in pieces if i):
        pieces[i] = after(pieces[i], done) if i == len(pieces) - 1 else pieces[i]
        done = take(i)


def hop(value, step, planes, *wait):
    me = lax.axis_index("gc")
    pairs = [(i, i + step) for i in range(0, planes, 2 * step)]
    came = after(lax.ppermute(value, "gc", pairs), *wait)
    return jnp.where(me % (2 * step) == step, came, value)


def steps_of(planes):
    return [planes >> i for i in range(1, planes.bit_length())]


def shards(child_rows, row_map, stair):
    groups, planes = lax.axis_size("gr"), lax.axis_size("gc")
    me, plane = lax.axis_index("gr"), lax.axis_index("gc")
    core = me & 1
    rows_dev, cols_dev = child_rows.shape
    panels = NPANEL * PANEL
    half = cols_dev // 2
    blocks = panels // EDGE
    base = 3 * rows_dev // (4 * groups)
    columns = jnp.arange(cols_dev, dtype=jnp.int32)
    stair_ids = jnp.arange(stair.shape[0], dtype=jnp.int32)
    child_limits = jnp.sum(
        jnp.where((row_map // STAIR_BLOCK)[:, None] == stair_ids[None, :], stair[None, :], 0), axis=1
    )
    child_limits = child_limits - plane * cols_dev
    own_blocks = rows_dev // STAIR_BLOCK
    limits = jnp.repeat(
        lax.dynamic_slice_in_dim(stair, me * own_blocks, own_blocks, 0), STAIR_BLOCK
    )
    limits = limits - plane * cols_dev
    everyone = range(planes)

    panel = jnp.where(columns[None, :panels] >= child_limits[:, None], child_rows[:, :panels], 0.0)
    pair = jnp.concatenate([panel, swap(panel)], axis=0)


    quarter = panels // 4
    outer = jnp.concatenate([pair[:, :quarter], pair[:, 3 * quarter :]], axis=1)
    share = jnp.where(core == 0, outer, pair[:, quarter : 3 * quarter])
    gram = dot(share, pair, ((0,), (0,)), HIGHEST)
    packed = []
    for lead in (0, blocks // 4):
        rows = []
        for i in range(blocks // 4):
            one, two = lead + i + 1, blocks - lead - i
            last = blocks // 2 - 1 - i
            rows.append(
                jnp.concatenate(
                    [
                        gram[i * EDGE : (i + 1) * EDGE, : one * EDGE],
                        gram[last * EDGE : (last + 1) * EDGE, : two * EDGE],
                    ],
                    axis=1,
                )
            )
        packed.append(jnp.concatenate(rows, axis=0))
    gram = jnp.where(core == 0, packed[0], packed[1])
    gram_sum = reduce_direct(gram, planes, [0])
    count = groups * base
    every = to_all(after(jnp.broadcast_to(row_map[None, :], (groups, rows_dev)), gram))
    pack_to = pack_plan(row_map, groups, rows_dev, base)
    part, late = cols_dev // groups, rows_dev - count
    joint = part % EDGE == 0 and cols_dev % panels == 0 and cols_dev > panels
    if joint:
        sent, rest = pack_both(child_rows, after(pack_to, gram), count, groups, panels)
        both = to_all(after(sent, gram_sum))
    else:
        direct, spread = pack(child_rows, after(pack_to, gram), count)
        spread = to_all(spread.reshape(late, groups, -1).transpose(1, 0, 2))
        direct = to_all(direct.reshape(groups, base, cols_dev)).reshape(count, cols_dev)
    steps = steps_of(planes)
    gram_first, everywhere = gram_sum, panel
    for step in steps:
        gram_first = hop(gram_first, step, planes)
        if step > 1:
            everywhere = hop(everywhere, step, planes, gram_first)

    turn_to, place_to = arrival_plan(every, rows_dev, base)
    turn_to, place_to = lax.optimization_barrier((turn_to, place_to))
    if joint:
        both = after(both, everywhere)
        spread = turn_both(both, turn_to, late, part).reshape(groups, late, part)
    else:
        spread = turn_rows(spread, turn_to)

    halves = []
    child = after(child_rows, gram_first)
    for start in (core * half, (1 - core) * half):
        value = lax.dynamic_slice_in_dim(child, start, half, 1)
        halves.append(jnp.where(start + columns[None, :half] >= child_limits[:, None], value, 0.0))
    other = swap(halves[1])
    gram = gather_direct(gram_first, planes, (spread, halves[0], halves[1]))
    grams = [jnp.stack([core, me // 2]).astype(jnp.int32), gram, swap(gram)]
    spread = to_all(spread)

    everywhere = hop(everywhere, 1, planes, gram, spread)
    spread = spread.transpose(1, 0, 2).reshape(late, cols_dev)
    if joint:
        front, own_panel = place_both(both, spread, place_to, limits, base, panels)
    else:
        front, own_panel = place(direct, spread, place_to, limits, None, 0)
        own_panel = own_panel[:, :panels]

    product = dot(halves[0], after(everywhere, own_panel), ((0,), (0,)), HIGH)
    product += dot(other, swap(everywhere), ((0,), (0,)), HIGH)
    product, came = send_stage(pieces_of(product), 0)
    grams = after(grams, own_panel, *product.values())
    inverse = inverse_factor(grams, panels, 0, blocks // 2, groups // 2)
    came[0] = after(came[0], inverse)
    own_panel = hop(own_panel, steps[0], planes, came[0])
    came[1:] = after(came[1:], came[0])
    stages = groups.bit_length() - 2
    product = add_stage(product, came)
    sent = send_stage(product, 1) if stages > 1 else None
    if joint:
        second = after(rest, product[max(product)])
        second = to_all(second.reshape(groups, base, -1)).reshape(count, -1)
    inverse = inverse_factor(
        [after(inverse, own_panel, product[max(product)])], panels, blocks // 2, blocks, groups // 2
    )
    for j in range(1, stages):
        left, came = sent if j == 1 else send_stage(product, j)
        product = add_stage(left, [after(one, inverse) for one in came])
    product = product[0]
    for step in steps[1:]:
        own_panel = hop(own_panel, step, planes, inverse)
    coupling = dot(inverse, product, ((1,), (1,)), HIGH)
    basis = basis_of(own_panel, inverse)
    if joint:
        (front,) = place(second, spread, after(place_to, coupling), limits, front, panels)
    piece_cols = coupling.shape[1]
    if piece_cols % EDGE == 0:
        held = [front, None]

        def use(pieces, where):
            held[:] = project(held[0], held[1], basis, pieces, where, me)
            return held[1]

        gather_pieces(coupling, use)
        return (held[1], held[0])
    held = [jnp.zeros((panels, cols_dev), jnp.float32)]

    def keep(pieces, where):
        for piece, at in zip(pieces, where):
            held[0] = lax.dynamic_update_slice_in_dim(held[0], piece, at * piece_cols, 1)
        return pieces[0]

    gather_pieces(coupling, keep)
    whole = held[0]
    share_rows = panels // groups
    factor = lax.dynamic_slice_in_dim(whole, me * share_rows, share_rows, 0)
    basis = basis[0].astype(jnp.float32) + basis[1].astype(jnp.float32)
    return (factor, front - dot(basis, whole, ((1,), (0,)), HIGH))


def solution(mesh):
    placed = (P("gr", "gc"), P("gr"), P())
    return jax.shard_map(
        shards,
        mesh=mesh,
        in_specs=placed,
        out_specs=(P("gr", "gc"), P("gr", "gc")),
        check_vma=False,
    )
```

```python
import functools

import jax
import jax.numpy as jnp
from jax import lax
from jax.experimental import pallas as pl
from jax.experimental.pallas import tpu as pltpu
from jax.sharding import PartitionSpec as P

PANEL = 512
NPANEL = 2
STAIR_BLOCK = 128
EDGE = 128
HIGHEST = lax.Precision.HIGHEST
HIGH = lax.Precision.HIGH


def dot(left, right, dims, precision):
    return lax.dot_general(
        left, right, (dims, ((), ())), precision=precision, preferred_element_type=jnp.float32
    )


def split(value):
    high = value.astype(jnp.bfloat16)
    return high, (value - high.astype(jnp.float32)).astype(jnp.bfloat16)


def triple(left, right, dims):
    small = dot(left[0], right[1], dims, None) + dot(left[1], right[0], dims, None)
    return small + dot(left[0], right[0], dims, None)


def eliminate(tiles):
    lane = lax.broadcasted_iota(jnp.int32, (8, EDGE), 1)
    sub = lax.broadcasted_iota(jnp.int32, (8, EDGE), 0)
    tiles = list(tiles)
    strips = len(tiles)
    for strip in range(strips):
        first = 8 * strip
        own = (lane >= first) & (lane < first + 8)
        mult = {
            t: [jnp.broadcast_to(tiles[t][:, first + s : first + s + 1], (8, EDGE)) for s in range(8)]
            for t in range(strip, strips)
        }
        small = [
            [jnp.broadcast_to(mult[strip][s][t : t + 1, :], (8, EDGE)) for s in range(t + 1)]
            for t in range(8)
        ]
        start = jnp.where(own, jnp.where(lane - first == sub, 1.0, 0.0), tiles[strip])
        rows = [jnp.broadcast_to(start[s : s + 1, :], (8, EDGE)) for s in range(8)]
        inv = [None] * 8
        low = [[None] * 8 for _ in range(8)]
        for s in range(8):
            inv[s] = 1.0 / small[s][s]
            for t in range(s + 1, 8):
                low[t][s] = small[t][s] * inv[s]
                for u in range(s + 1, t + 1):
                    small[t][u] = small[t][u] - low[t][s] * small[u][s]
            for t in range(s + 1, 8):
                rows[t] = rows[t] - low[t][s] * rows[s]
        back = [None] * 8
        for s in range(7, -1, -1):
            value = rows[s] * inv[s]
            for t in range(7, s, -1):
                value = value - low[t][s] * back[t]
            back[s] = value
        out, pivot = rows[7], small[7][7]
        for s in range(6, -1, -1):
            out = jnp.where(sub == s, rows[s], out)
            pivot = jnp.where(sub == s, small[s][s], pivot)
        tiles[strip] = out * lax.rsqrt(pivot)
        for t in range(strip + 1, strips):
            value = jnp.where(own, 0.0, tiles[t])
            for s in range(8):
                value = value - mult[t][s] * back[s]
            tiles[t] = value
    return tiles


def unpack(where_ref, chips, halves, work):
    size = work.shape[0]
    blocks = size // EDGE
    for which, half in enumerate(halves):
        core = where_ref[0] ^ which
        rows = half.shape[0] // chips
        for r in range(chips):
            first = (where_ref[1] ^ r) * rows
            pair = core * (blocks // 4) + first // EDGE
            inside = first % EDGE
            for b in range(blocks + 1):
                lead = b <= pair
                row = jnp.where(lead, pair, blocks - 1 - pair)
                col = jnp.where(lead, b, b - pair - 1)
                work[
                    pl.ds(pl.multiple_of(row * EDGE + inside, 8), rows),
                    pl.ds(pl.multiple_of(col * EDGE, EDGE), EDGE),
                ] = half[r * rows : (r + 1) * rows, b * EDGE : (b + 1) * EDGE]
    for i in range(blocks):
        for j in range(i):
            work[j * EDGE : (j + 1) * EDGE, i * EDGE : (i + 1) * EDGE] = work[
                i * EDGE : (i + 1) * EDGE, j * EDGE : (j + 1) * EDGE
            ].T


def inverse_factor_kernel(first, last, chips, *refs):
    out_ref, work, high, low = refs[-4:]
    size = work.shape[0]
    blocks = size // EDGE
    if first == 0:
        unpack(refs[0], chips, refs[1:-4], work)
    else:
        work[...] = refs[0][...]
    lower = lax.broadcasted_iota(jnp.int32, (EDGE, EDGE), 0) >= lax.broadcasted_iota(
        jnp.int32, (EDGE, EDGE), 1
    )

    @pl.loop(first, last)
    def _(k):
        at = pl.multiple_of(k * EDGE, EDGE)
        tiles = [
            work[pl.ds(pl.multiple_of(at + 8 * t, 8), 8), pl.ds(at, EDGE)] for t in range(EDGE // 8)
        ]
        diag = jnp.where(lower, jnp.concatenate(eliminate(tiles), axis=0), 0.0)
        work[pl.ds(at, EDGE), :] = triple(split(diag), split(work[pl.ds(at, EDGE), :]), ((1,), (0,)))
        work[pl.ds(at, EDGE), pl.ds(at, EDGE)] = diag
        high[...], low[...] = split(work[pl.ds(at, EDGE), :])

        @pl.loop(k + 1, blocks)
        def _(i):
            below = pl.multiple_of(i * EDGE, EDGE)
            coeff = high[:, pl.ds(below, EDGE)], low[:, pl.ds(below, EDGE)]
            work[pl.ds(below, EDGE), pl.ds(at, EDGE)] = jnp.zeros((EDGE, EDGE), jnp.float32)
            work[pl.ds(below, EDGE), :] -= triple(coeff, (high[...], low[...]), ((0,), (0,)))

    if last == blocks:
        for k in range(blocks - 1):
            work[k * EDGE : (k + 1) * EDGE, (k + 1) * EDGE :] = jnp.zeros(
                (EDGE, size - (k + 1) * EDGE), jnp.float32
            )
    out_ref[...] = work[...]


def inverse_factor(held, size, first, last, chips):
    vmem = pl.BlockSpec(memory_space=pltpu.VMEM)
    specs = [vmem] if first else [pl.BlockSpec(memory_space=pltpu.SMEM), vmem, vmem]
    return pl.pallas_call(
        functools.partial(inverse_factor_kernel, first, last, chips),
        out_shape=jax.ShapeDtypeStruct((size, size), jnp.float32),
        in_specs=specs,
        out_specs=vmem,
        scratch_shapes=[pltpu.VMEM((size, size), jnp.float32)]
        + [pltpu.VMEM((EDGE, size), jnp.bfloat16)] * 2,
        compiler_params=pltpu.CompilerParams(vmem_limit_bytes=40 * 2**20),
        cost_estimate=pl.CostEstimate(
            flops=32 * size**3, bytes_accessed=32 * size * size, transcendentals=size
        ),
        name="inverse_factor",
    )(*held)


def pick(where_to, count):
    rows = lax.broadcasted_iota(jnp.int32, (count, where_to.shape[1]), 0)
    return jnp.where(rows == where_to, 1.0, 0.0).astype(jnp.bfloat16)


def move(matrix, values):
    high = values.astype(jnp.bfloat16)
    rest = (values - high.astype(jnp.float32)).astype(jnp.bfloat16)
    dims = ((1,), (0,))
    return dot(matrix, high, dims, None) + dot(matrix, rest, dims, None)


def reorder_kernel(to_ref, in_ref, out_ref, matrix):
    matrix[...] = pick(to_ref[...], matrix.shape[0])
    out_ref[...] = move(matrix[...], in_ref[...])


def reorder(values, where_to):
    count, width = values.shape
    return pl.pallas_call(
        reorder_kernel,
        out_shape=jax.ShapeDtypeStruct((count, width), jnp.float32),
        in_specs=[pl.BlockSpec(memory_space=pltpu.VMEM)] * 2,
        out_specs=pl.BlockSpec(memory_space=pltpu.VMEM),
        scratch_shapes=[pltpu.VMEM((count, count), jnp.bfloat16)],
        compiler_params=pltpu.CompilerParams(vmem_limit_bytes=40 * 2**20),
        cost_estimate=pl.CostEstimate(
            flops=4 * count * count * width, bytes_accessed=8 * count * width, transcendentals=0
        ),
        name="reorder",
    )(where_to.reshape(1, count), values)


def block_width(width):
    for block in (512, 384, 256, 128):
        if width % block == 0:
            return block
    return width


def pack_kernel(to_ref, in_ref, direct_ref, other_ref, matrix):
    @pl.when(pl.program_id(0) == 0)
    def _():
        matrix[...] = pick(to_ref[...], matrix.shape[0])

    count = direct_ref.shape[0]
    value = move(matrix[...], in_ref[...])
    direct_ref[...] = value[:count]
    other_ref[...] = value[count:]


def pack(values, where_to, count):
    rows, width = values.shape
    block = block_width(width)
    return pl.pallas_call(
        pack_kernel,
        grid=(width // block,),
        out_shape=[
            jax.ShapeDtypeStruct((count, width), jnp.float32),
            jax.ShapeDtypeStruct((rows - count, width), jnp.float32),
        ],
        in_specs=[
            pl.BlockSpec((1, rows), lambda j: (0, 0)),
            pl.BlockSpec((rows, block), lambda j: (0, j)),
        ],
        out_specs=[
            pl.BlockSpec((count, block), lambda j: (0, j)),
            pl.BlockSpec((rows - count, block), lambda j: (0, j)),
        ],
        scratch_shapes=[pltpu.VMEM((rows, rows), jnp.bfloat16)],
        compiler_params=pltpu.CompilerParams(vmem_limit_bytes=40 * 2**20),
        cost_estimate=pl.CostEstimate(
            flops=4 * rows * rows * width, bytes_accessed=8 * rows * width, transcendentals=0
        ),
        name="pack",
    )(where_to.reshape(1, rows), values)


def place_kernel(offset, outs, to_ref, limit_ref, direct_ref, other_ref, *rest):
    out_refs, matrix = rest[len(rest) - 1 - outs : -1], rest[-1]
    block = pl.program_id(0)

    @pl.when(block == 0)
    def _():
        matrix[...] = pick(to_ref[...], matrix.shape[0])

    count = direct_ref.shape[0]
    value = move(matrix[:, :count], direct_ref[...]) + move(matrix[:, count:], other_ref[...])
    column = lax.broadcasted_iota(jnp.int32, value.shape, 1) + (block + offset) * value.shape[1]
    for out_ref in out_refs:
        out_ref[...] = jnp.where(column >= limit_ref[...], value, 0.0)


def place(direct, other, where_to, limits, front, start):
    rows = limits.shape[0]
    width, full = direct.shape[1], other.shape[1]
    block = block_width(width)
    offset = start // block
    held = [] if front is None else [front]
    outs = [jax.ShapeDtypeStruct((rows, full), jnp.float32)]
    out_specs = [pl.BlockSpec((rows, block), lambda j: (0, j + offset))]
    if not held:
        outs.append(jax.ShapeDtypeStruct((rows, width), jnp.float32))
        out_specs.append(pl.BlockSpec((rows, block), lambda j: (0, j)))
    return pl.pallas_call(
        functools.partial(place_kernel, offset, len(outs)),
        grid=(width // block,),
        out_shape=outs,
        in_specs=[
            pl.BlockSpec((1, rows), lambda j: (0, 0)),
            pl.BlockSpec((rows, 1), lambda j: (0, 0)),
            pl.BlockSpec((direct.shape[0], block), lambda j: (0, j)),
            pl.BlockSpec((other.shape[0], block), lambda j: (0, j + offset)),
        ]
        + [pl.BlockSpec(memory_space=pl.ANY) for _ in held],
        out_specs=out_specs,
        scratch_shapes=[pltpu.VMEM((rows, rows), jnp.bfloat16)],
        input_output_aliases={4: 0} if held else {},
        compiler_params=pltpu.CompilerParams(vmem_limit_bytes=40 * 2**20),
        cost_estimate=pl.CostEstimate(
            flops=4 * rows * rows * width, bytes_accessed=8 * rows * width, transcendentals=0
        ),
        name="place",
    )(where_to.reshape(1, rows), limits.reshape(rows, 1), direct, other, *held)


def pack_both_kernel(to_ref, in_ref, both_ref, rest_ref, matrix):
    block = pl.program_id(0)

    @pl.when(block == 0)
    def _():
        matrix[...] = pick(to_ref[...], matrix.shape[0])

    groups = both_ref.shape[0]
    count, width = rest_ref.shape
    late = in_ref.shape[0] - count
    base = count // groups
    inner = width // EDGE
    value = move(matrix[...], in_ref[...])
    blocks = pl.num_programs(0) * inner // groups
    first = both_ref.shape[1] - late * blocks
    panel_steps = first // base // inner

    @pl.when(block < panel_steps)
    def _():
        for d in range(groups):
            for c in range(inner):
                at = pl.multiple_of((block * inner + c) * base, 8)
                both_ref[d, pl.ds(at, base), :] = value[
                    d * base : (d + 1) * base, c * EDGE : (c + 1) * EDGE
                ]

    @pl.when(block >= panel_steps)
    def _():
        rest_ref[...] = value[:count]

    for c in range(inner):
        at = block * inner + c
        row = pl.multiple_of(first + lax.rem(at, blocks) * late, 8)
        both_ref[lax.div(at, blocks), pl.ds(row, late), :] = value[count:, c * EDGE : (c + 1) * EDGE]


def pack_both(values, where_to, count, groups, panels):
    rows, full = values.shape
    block = block_width(panels)
    steps = panels // block
    size = (count // groups) * (panels // EDGE) + (rows - count) * (full // groups // EDGE)
    return pl.pallas_call(
        pack_both_kernel,
        grid=(full // block,),
        out_shape=[
            jax.ShapeDtypeStruct((groups, size, EDGE), jnp.float32),
            jax.ShapeDtypeStruct((count, full - panels), jnp.float32),
        ],
        in_specs=[
            pl.BlockSpec((1, rows), lambda j: (0, 0)),
            pl.BlockSpec((rows, block), lambda j: (0, j)),
        ],
        out_specs=[
            pl.BlockSpec((groups, size, EDGE), lambda j: (0, 0, 0)),
            pl.BlockSpec((count, block), lambda j: (0, jnp.maximum(j - steps, 0))),
        ],
        scratch_shapes=[pltpu.VMEM((rows, rows), jnp.bfloat16)],
        compiler_params=pltpu.CompilerParams(vmem_limit_bytes=40 * 2**20),
        cost_estimate=pl.CostEstimate(
            flops=4 * rows * rows * full, bytes_accessed=8 * rows * full, transcendentals=0
        ),
        name="pack_both",
    )(where_to.reshape(1, rows), values)


def turn_both_kernel(to_ref, in_ref, out_ref, matrix):
    matrix[...] = pick(to_ref[...], matrix.shape[0])
    groups = in_ref.shape[0]
    late = out_ref.shape[0] // groups
    blocks = out_ref.shape[1] // EDGE
    first = in_ref.shape[1] - late * blocks
    for c in range(blocks):
        at = first + c * late
        value = jnp.concatenate([in_ref[h, at : at + late, :] for h in range(groups)], axis=0)
        out_ref[:, c * EDGE : (c + 1) * EDGE] = move(matrix[...], value)


def turn_both(both, where_to, late, part):
    groups = both.shape[0]
    count = groups * late
    vmem = pl.BlockSpec(memory_space=pltpu.VMEM)
    return pl.pallas_call(
        turn_both_kernel,
        out_shape=jax.ShapeDtypeStruct((count, part), jnp.float32),
        in_specs=[vmem] * 2,
        out_specs=vmem,
        scratch_shapes=[pltpu.VMEM((count, count), jnp.bfloat16)],
        compiler_params=pltpu.CompilerParams(vmem_limit_bytes=40 * 2**20),
        cost_estimate=pl.CostEstimate(
            flops=4 * count * count * part, bytes_accessed=8 * count * part, transcendentals=0
        ),
        name="turn_both",
    )(where_to.reshape(1, count), both)


def place_both_kernel(base, to_ref, limit_ref, both_ref, other_ref, out_ref, panel_ref, matrix):
    block = pl.program_id(0)

    @pl.when(block == 0)
    def _():
        matrix[...] = pick(to_ref[...], matrix.shape[0])

    groups = both_ref.shape[0]
    count = groups * base
    inner = out_ref.shape[1] // EDGE
    for c in range(inner):
        at = pl.multiple_of((block * inner + c) * base, 8)
        own = slice(c * EDGE, (c + 1) * EDGE)
        direct = jnp.concatenate([both_ref[h, pl.ds(at, base), :] for h in range(groups)], axis=0)
        value = move(matrix[:, :count], direct) + move(matrix[:, count:], other_ref[:, own])
        column = lax.broadcasted_iota(jnp.int32, value.shape, 1) + (block * inner + c) * EDGE
        value = jnp.where(column >= limit_ref[...], value, 0.0)
        out_ref[:, own] = value
        panel_ref[:, own] = value


def place_both(both, other, where_to, limits, base, panels):
    rows, full = limits.shape[0], other.shape[1]
    block = block_width(panels)
    return pl.pallas_call(
        functools.partial(place_both_kernel, base),
        grid=(panels // block,),
        out_shape=[
            jax.ShapeDtypeStruct((rows, full), jnp.float32),
            jax.ShapeDtypeStruct((rows, panels), jnp.float32),
        ],
        in_specs=[
            pl.BlockSpec((1, rows), lambda j: (0, 0)),
            pl.BlockSpec((rows, 1), lambda j: (0, 0)),
            pl.BlockSpec(both.shape, lambda j: (0, 0, 0)),
            pl.BlockSpec((other.shape[0], block), lambda j: (0, j)),
        ],
        out_specs=[pl.BlockSpec((rows, block), lambda j: (0, j))] * 2,
        scratch_shapes=[pltpu.VMEM((rows, rows), jnp.bfloat16)],
        compiler_params=pltpu.CompilerParams(vmem_limit_bytes=40 * 2**20),
        cost_estimate=pl.CostEstimate(
            flops=4 * rows * rows * panels, bytes_accessed=8 * rows * panels, transcendentals=0
        ),
        name="place_both",
    )(where_to.reshape(1, rows), limits.reshape(rows, 1), both, other)


def basis_kernel(panel_ref, inverse_ref, high_ref, low_ref):
    value = triple(split(panel_ref[...]), split(inverse_ref[...]), ((1,), (1,)))
    high_ref[...], low_ref[...] = split(value)


def basis_of(panel, inverse):
    rows, panels = panel.shape
    vmem = pl.BlockSpec(memory_space=pltpu.VMEM)
    return pl.pallas_call(
        basis_kernel,
        out_shape=[jax.ShapeDtypeStruct((rows, panels), jnp.bfloat16)] * 2,
        in_specs=[vmem] * 2,
        out_specs=[vmem] * 2,
        compiler_params=pltpu.CompilerParams(vmem_limit_bytes=56 * 2**20),
        cost_estimate=pl.CostEstimate(
            flops=6 * rows * panels * panels,
            bytes_accessed=4 * panels * (2 * rows + panels),
            transcendentals=0,
        ),
        name="basis",
    )(panel, inverse)


def project_kernel(count, last, where_ref, high_ref, low_ref, front_ref, *rest):
    pieces, (out_ref, factor_ref) = rest[:count], rest[-2:]
    step = pl.program_id(0)
    share = factor_ref.shape[0]
    own = pl.ds(pl.multiple_of(where_ref[last] * share, share), share)
    for i in range(count):

        @pl.when(step == i)
        def _():
            factor_ref[...] = pieces[i][own, :]
            update = triple((high_ref[...], low_ref[...]), split(pieces[i][...]), ((1,), (0,)))
            out_ref[...] = front_ref[...] - update


def project(front, factor, basis, pieces, table, first):
    rows, full = front.shape
    panels, width = pieces[0].shape
    count = len(pieces)
    share = panels // lax.axis_size("gr")
    last = table.shape[0] - 1
    held = [] if factor is None else [factor]
    whole = pl.BlockSpec((rows, panels), lambda j, at: (0, 0))
    block = pl.BlockSpec((rows, width), lambda j, at: (0, at[first + j]))
    return pl.pallas_call(
        functools.partial(project_kernel, count, last),
        grid_spec=pltpu.PrefetchScalarGridSpec(
            num_scalar_prefetch=1,
            grid=(count,),
            in_specs=[whole, whole, block]
            + [pl.BlockSpec((panels, width), lambda j, at: (0, 0)) for _ in pieces]
            + [pl.BlockSpec(memory_space=pl.ANY) for _ in held],
            out_specs=[block, pl.BlockSpec((share, width), lambda j, at: (0, at[first + j]))],
        ),
        out_shape=[
            jax.ShapeDtypeStruct((rows, full), jnp.float32),
            jax.ShapeDtypeStruct((share, full), jnp.float32),
        ],
        input_output_aliases={3: 0, 4 + count: 1} if held else {3: 0},
        compiler_params=pltpu.CompilerParams(vmem_limit_bytes=56 * 2**20),
        cost_estimate=pl.CostEstimate(
            flops=6 * rows * panels * width * count,
            bytes_accessed=4 * count * (2 * rows + panels) * width,
            transcendentals=0,
        ),
        name="project",
    )(table, *basis, front, *pieces, *held)


def pack_plan(row_map, groups, rows_dev, base):
    dest = row_map // rows_dev
    at = jnp.arange(rows_dev, dtype=jnp.int32)
    before = (at[:, None] < at[None, :]).astype(jnp.bfloat16)
    onehot = dest[None, :] == jnp.arange(groups, dtype=jnp.int32)[:, None]
    ahead = dot(onehot.astype(jnp.bfloat16), before, ((1,), (0,)), None)
    rank = jnp.sum(jnp.where(onehot, ahead, 0.0), axis=0).astype(jnp.int32)
    late = rank >= base
    late_rank = dot(late[None, :].astype(jnp.bfloat16), before, ((1,), (0,)), None)[0]
    return jnp.where(late, groups * base + late_rank.astype(jnp.int32), dest * base + rank)


def arrival_plan(every, rows_dev, base):
    me = lax.axis_index("gr")
    groups = every.shape[0]
    other = rows_dev - groups * base
    dest, slot = every // rows_dev, every % rows_dev
    at = jnp.arange(rows_dev, dtype=jnp.int32)
    before = (at[:, None] < at[None, :]).astype(jnp.bfloat16)
    group_ids = jnp.arange(groups, dtype=jnp.int32)
    onehot = dest[:, None, :] == group_ids[None, :, None]
    ahead = dot(
        onehot.reshape(groups * groups, rows_dev).astype(jnp.bfloat16), before, ((1,), (0,)), None
    ).reshape(groups, groups, rows_dev)
    rank = jnp.sum(jnp.where(onehot, ahead, 0.0), axis=1).astype(jnp.int32)
    late = rank >= base
    late_rank = dot(late.astype(jnp.bfloat16), before, ((1,), (0,)), None).astype(jnp.int32)
    sent = jnp.sum(onehot.astype(jnp.int32), axis=2) - base
    earlier = jnp.cumsum(sent, axis=0) - sent
    start = jnp.sum(jnp.where(onehot, earlier[:, :, None], 0), axis=1)
    turn = start + rank - base
    late_ids = jnp.arange(other, dtype=jnp.int32)
    chosen = late[:, None, :] & (late_rank[:, None, :] == late_ids[None, :, None])
    turn_to = jnp.sum(jnp.where(chosen, (dest * other + turn)[:, None, :], 0), axis=2).reshape(-1)
    arrival = jnp.where(late, groups * base + turn, group_ids[:, None] * base + rank)
    arrival = jnp.where(dest == me, arrival, -1).reshape(-1)
    place_to = jnp.sum(
        jnp.where(arrival[None, :] == at[:, None], slot.reshape(-1)[None, :], 0), axis=1
    )
    return turn_to, place_to


def to_all(value):
    return lax.all_to_all(value, "gr", 0, 0, tiled=True)


def turn_rows(spread, turn_to):
    groups, other, part = spread.shape
    return reorder(spread.reshape(groups * other, part), turn_to).reshape(groups, other, part)


def after(value, *others):
    if isinstance(value, (list, tuple)):
        return list(lax.optimization_barrier(tuple(value) + others)[: len(value)])
    return lax.optimization_barrier((value,) + others)[0]


def stages_of(groups, core):
    count = groups.bit_length() - 1
    me = lax.axis_index("gr")
    found = []
    for one, two in zip(range(1, count), range(count - 1, 0, -1)):
        pairs = [(i, i ^ (1 << (two if i & 1 else one))) for i in range(groups)]
        found.append((pairs, jnp.where(core == 1, (me >> two) & 1, (me >> one) & 1)))
    return found


def swap(value):
    groups = lax.axis_size("gr")
    return lax.ppermute(value, "gr", [(i, i ^ 1) for i in range(groups)])


def position(index, stages, core):
    at = core
    for j, (_, mine) in enumerate(stages):
        at = 2 * at + (mine ^ ((index >> (len(stages) - 1 - j)) & 1))
    return at


def chip_pairs(r, planes, chosen):
    groups = lax.axis_size("gr")
    return [
        (i * planes + z, (i ^ (2 * r)) * planes + z) for i in range(groups) for z in chosen
    ]


def reduce_direct(value, planes, chosen):
    chips = lax.axis_size("gr") // 2
    chip = lax.axis_index("gr") // 2
    size = value.shape[0] // chips

    def rows_of(r):
        return lax.dynamic_slice_in_dim(value, (chip ^ r) * size, size, 0)

    came = [
        lax.ppermute(rows_of(r), ("gr", "gc"), chip_pairs(r, planes, chosen))
        for r in range(chips - 1, 0, -1)
    ]
    total = rows_of(0)
    for one in came:
        total = total + one
    return total


def gather_direct(value, planes, wait):
    chips = lax.axis_size("gr") // 2
    every = range(planes)
    came = [
        lax.ppermute(value, ("gr", "gc"), chip_pairs(r, planes, every)) for r in range(1, chips)
    ]
    came = after(came, *wait)
    return jnp.concatenate([value] + came, axis=0)


def send_stage(pieces, j):
    groups = lax.axis_size("gr")
    stages = stages_of(groups, lax.axis_index("gr") & 1)
    bit = 1 << (len(stages) - 1 - j)
    order = sorted((i for i in pieces if i & bit), reverse=True)
    came = [lax.ppermute(pieces[i], "gr", stages[j][0]) for i in reversed(order)][::-1]
    return {i ^ bit: pieces[i ^ bit] for i in order}, came


def add_stage(left, came):
    return {i: left[i] + one for i, one in zip(left, came)}


def pieces_of(value):
    stages = stages_of(lax.axis_size("gr"), lax.axis_index("gr") & 1)
    size = value.shape[0] >> len(stages)
    return {
        i: lax.dynamic_slice_in_dim(value, position(i, stages, jnp.int32(0)) * size, size, 0)
        for i in range(1 << len(stages))
    }


def gather_pieces(piece, use):
    core = lax.axis_index("gr") & 1
    stages, others = stages_of(lax.axis_size("gr"), core), stages_of(lax.axis_size("gr"), 1 - core)
    pieces = {0: piece}

    table = []
    for i in range(1 << len(stages)):
        table += [position(i, stages, core), position(i, others, 1 - core)]
    table = jnp.stack(table + [lax.axis_index("gr")]).astype(jnp.int32)

    def take(numbers):
        held = []
        for i in numbers:
            held += [pieces[i], swap(pieces[i])]
        return held, table, 2 * numbers[0]

    for j in range(len(stages) - 1, -1, -1):
        bit = 1 << (len(stages) - 1 - j)
        pieces[bit] = lax.ppermute(piece, "gr", stages[j][0])
    done = use(*take([0]))
    for i in pieces:
        pieces[i] = after(pieces[i], done)
    for j in range(len(stages) - 2, -1, -1):
        bit = 1 << (len(stages) - 1 - j)
        for i in range(1, bit):
            pieces[i | bit] = lax.ppermute(pieces[i], "gr", stages[j][0])
    last = max(pieces)
    done = use(*take(sorted(i for i in pieces if 0 < i < last)))
    pieces[last] = after(pieces[last], done)
    held, table, first = take([last])
    for i, one in enumerate(held):
        use([one], table, first + i)


def hop(value, step, planes, *wait):
    me = lax.axis_index("gc")
    pairs = [(i, i + step) for i in range(0, planes, 2 * step)]
    came = after(lax.ppermute(value, "gc", pairs), *wait)
    return jnp.where(me % (2 * step) == step, came, value)


def steps_of(planes):
    return [planes >> i for i in range(1, planes.bit_length())]


def shards(child_rows, row_map, stair):
    groups, planes = lax.axis_size("gr"), lax.axis_size("gc")
    me, plane = lax.axis_index("gr"), lax.axis_index("gc")
    core = me & 1
    rows_dev, cols_dev = child_rows.shape
    panels = NPANEL * PANEL
    half = cols_dev // 2
    blocks = panels // EDGE
    base = 3 * rows_dev // (4 * groups)
    columns = jnp.arange(cols_dev, dtype=jnp.int32)
    stair_ids = jnp.arange(stair.shape[0], dtype=jnp.int32)
    child_limits = jnp.sum(
        jnp.where((row_map // STAIR_BLOCK)[:, None] == stair_ids[None, :], stair[None, :], 0), axis=1
    )
    child_limits = child_limits - plane * cols_dev
    own_blocks = rows_dev // STAIR_BLOCK
    limits = jnp.repeat(
        lax.dynamic_slice_in_dim(stair, me * own_blocks, own_blocks, 0), STAIR_BLOCK
    )
    limits = limits - plane * cols_dev
    everyone = range(planes)

    panel = jnp.where(columns[None, :panels] >= child_limits[:, None], child_rows[:, :panels], 0.0)
    pair = jnp.concatenate([panel, swap(panel)], axis=0)


    quarter = panels // 4
    outer = jnp.concatenate([pair[:, :quarter], pair[:, 3 * quarter :]], axis=1)
    share = jnp.where(core == 0, outer, pair[:, quarter : 3 * quarter])
    gram = dot(share, pair, ((0,), (0,)), HIGHEST)
    packed = []
    for lead in (0, blocks // 4):
        rows = []
        for i in range(blocks // 4):
            one, two = lead + i + 1, blocks - lead - i
            last = blocks // 2 - 1 - i
            rows.append(
                jnp.concatenate(
                    [
                        gram[i * EDGE : (i + 1) * EDGE, : one * EDGE],
                        gram[last * EDGE : (last + 1) * EDGE, : two * EDGE],
                    ],
                    axis=1,
                )
            )
        packed.append(jnp.concatenate(rows, axis=0))
    gram = jnp.where(core == 0, packed[0], packed[1])
    gram_sum = reduce_direct(gram, planes, [0])
    count = groups * base
    every = to_all(after(jnp.broadcast_to(row_map[None, :], (groups, rows_dev)), gram))
    pack_to = pack_plan(row_map, groups, rows_dev, base)
    part, late = cols_dev // groups, rows_dev - count
    joint = part % EDGE == 0 and cols_dev % panels == 0 and cols_dev > panels
    if joint:
        sent, rest = pack_both(child_rows, after(pack_to, gram), count, groups, panels)
        both = to_all(after(sent, gram_sum))
    else:
        direct, spread = pack(child_rows, after(pack_to, gram), count)
        spread = to_all(spread.reshape(late, groups, -1).transpose(1, 0, 2))
        direct = to_all(direct.reshape(groups, base, cols_dev)).reshape(count, cols_dev)
    steps = steps_of(planes)
    gram_first, everywhere = gram_sum, panel
    for step in steps:
        gram_first = hop(gram_first, step, planes)
        if step > 1:
            everywhere = hop(everywhere, step, planes, gram_first)

    turn_to, place_to = arrival_plan(every, rows_dev, base)
    turn_to, place_to = lax.optimization_barrier((turn_to, place_to))
    if joint:
        both = after(both, everywhere)
        spread = turn_both(both, turn_to, late, part).reshape(groups, late, part)
    else:
        spread = turn_rows(spread, turn_to)

    halves = []
    child = after(child_rows, gram_first)
    for start in (core * half, (1 - core) * half):
        value = lax.dynamic_slice_in_dim(child, start, half, 1)
        halves.append(jnp.where(start + columns[None, :half] >= child_limits[:, None], value, 0.0))
    other = swap(halves[1])
    gram = gather_direct(gram_first, planes, (spread, halves[0], halves[1]))
    grams = [jnp.stack([core, me // 2]).astype(jnp.int32), gram, swap(gram)]
    spread = to_all(spread)

    everywhere = hop(everywhere, 1, planes, gram, spread)
    spread = spread.transpose(1, 0, 2).reshape(late, cols_dev)
    if joint:
        front, own_panel = place_both(both, spread, place_to, limits, base, panels)
    else:
        front, own_panel = place(direct, spread, place_to, limits, None, 0)
        own_panel = own_panel[:, :panels]

    product = dot(halves[0], after(everywhere, own_panel), ((0,), (0,)), HIGH)
    product += dot(other, swap(everywhere), ((0,), (0,)), HIGH)
    product, came = send_stage(pieces_of(product), 0)
    grams = after(grams, own_panel, *product.values())
    inverse = inverse_factor(grams, panels, 0, blocks // 2, groups // 2)
    came[0] = after(came[0], inverse)
    own_panel = hop(own_panel, steps[0], planes, came[0])
    came[1:] = after(came[1:], came[0])
    stages = groups.bit_length() - 2
    product = add_stage(product, came)
    sent = send_stage(product, 1) if stages > 1 else None
    if joint:
        second = after(rest, product[max(product)])
        second = to_all(second.reshape(groups, base, -1)).reshape(count, -1)
    inverse = inverse_factor(
        [after(inverse, own_panel, product[max(product)])], panels, blocks // 2, blocks, groups // 2
    )
    for j in range(1, stages):
        left, came = sent if j == 1 else send_stage(product, j)
        product = add_stage(left, [after(one, inverse) for one in came])
    product = product[0]
    for step in steps[1:]:
        own_panel = hop(own_panel, step, planes, inverse)
    coupling = dot(inverse, product, ((1,), (1,)), HIGH)
    basis = basis_of(own_panel, inverse)
    if joint:
        (front,) = place(second, spread, after(place_to, coupling), limits, front, panels)
    piece_cols = coupling.shape[1]
    if piece_cols % EDGE == 0:
        held = [front, None]

        def use(pieces, table, first):
            held[:] = project(held[0], held[1], basis, pieces, table, first)
            return held[1]

        gather_pieces(coupling, use)
        return (held[1], held[0])
    held = [jnp.zeros((panels, cols_dev), jnp.float32)]

    def keep(pieces, table, first):
        for i, piece in enumerate(pieces):
            at = table[first + i]
            held[0] = lax.dynamic_update_slice_in_dim(held[0], piece, at * piece_cols, 1)
        return pieces[0]

    gather_pieces(coupling, keep)
    whole = held[0]
    share_rows = panels // groups
    factor = lax.dynamic_slice_in_dim(whole, me * share_rows, share_rows, 0)
    basis = basis[0].astype(jnp.float32) + basis[1].astype(jnp.float32)
    return (factor, front - dot(basis, whole, ((1,), (0,)), HIGH))


def solution(mesh):
    placed = (P("gr", "gc"), P("gr"), P())
    return jax.shard_map(
        shards,
        mesh=mesh,
        in_specs=placed,
        out_specs=(P("gr", "gc"), P("gr", "gc")),
        check_vma=False,
    )
```
